256 devices in a mesh: bins: 128 (over z, x_hi, y, core), diag: 2 (over x_lo).
Axes of the slice: x: 4 (x_hi: 2, x_lo: 2; x = x_hi * 2 + x_lo), y: 4, z: 8, core: 2. Of those that a mesh axis runs over, the one named last changes fastest.
Arguments:
- features: bfloat16 [32, 192, 16384], P(None, 'diag', 'bins'), may hold values from -6 to 6
- cotangent: bfloat16 [32, 192, 16384], P(None, 'diag', 'bins'), may hold values from -6 to 6
- band_mask: int32 [192, 16384], P('diag', 'bins'), may hold values 0 or 1
- dilation: int32 [2], replicated, may hold values from 1 to 8, as said below
- w_first: bfloat16 [32, 9, 32], replicated, may hold values from -0.375 to 0.375
- b_first: float32 [32], replicated, may hold values from -3 to 3
- w_second: bfloat16 [32, 9, 32], replicated, may hold values from -0.375 to 0.375
Outputs:
- output: bfloat16 [32, 192, 16384], P(None, 'diag', 'bins')
- grad_features: bfloat16 [32, 192, 16384], P(None, 'diag', 'bins')
- grad_w_first: float32 [32, 9, 32], replicated
- grad_b_first: float32 [32], replicated
- grad_w_second: float32 [32, 9, 32], replicated
The draws below stay inside these ranges and needn't reach their ends.
Inputs may be any that keep to these rules, and one draw needn't show every extreme that they name: Entry k is the dilation rate of convolution k; one of the two equals 8.
All inputs are finite; a program needn't handle non-finite values. No bound on the sum of `band_mask` on one device may be relied on, other than what follows from the above.
Results may differ from the reference program's by a relative error of at most 0.013.
Values may be sent and summed in bfloat16 or wider, within the bound.
A program may use at most 128 MiB of HBM per device.

```python
import jax
import jax.numpy as jnp
from jax import lax

C = 32
OFF = 192
RMAX = 8
BIN_DEV = 128
NB = 16384
CELLS = 3145728


def draw_dilation(key, part):
    key = jax.random.fold_in(key, 11)
    first_key, second_key = jax.random.split(key)
    other_rate = jax.random.randint(first_key, (), 1, RMAX + 1)
    chosen = jax.random.randint(second_key, (), 0, 2)
    return jnp.where(jnp.arange(2) == chosen, RMAX, other_rate).astype(jnp.int32)


def place_ends(drawn, stream_key, low, high):
    spot = [jax.random.randint(jax.random.fold_in(stream_key, axis), (), 0, length) for axis, length in enumerate(drawn.shape)]
    longest = drawn.shape.index(max(drawn.shape))
    beside = spot[:longest] + [(spot[longest] + 1) % drawn.shape[longest]] + spot[longest + 1:]
    return drawn.at[tuple(spot)].set(low).at[tuple(beside)].set(high)


def block_scale(rng, dims, shards, low, high):
    gain = 1.0
    for position, blocks in shards:
        draws = jax.random.uniform(jax.random.fold_in(jax.random.fold_in(rng, 6), position), (blocks,), jnp.float32, low / len(shards), high / len(shards))
        gain = gain * jnp.repeat(jnp.exp(draws), dims[position] // blocks).reshape((-1,) + (1,) * (len(dims) - 1 - position))
    return gain


def noise(key, shape, spread, bound, cuts=(), kind=jnp.bfloat16):
    entries = spread * jax.random.normal(key, shape, jnp.float32)
    if cuts:
        entries = entries * block_scale(key, shape, cuts, -0.22, 0.18)
    return jnp.clip(entries, -bound, bound).astype(kind)


def setup_inputs(seed: int = 0) -> dict:
    key_of = jax.random.split(jax.random.key(seed), 8)
    features = noise(key_of[0], (C, OFF, NB), 1.0, 6.0, ((1, 2), (2, 128)))
    cotangent = noise(key_of[1], (C, OFF, NB), 1.0, 6.0, ((1, 2), (2, 128)))
    band_mask = place_ends((jax.random.randint(key_of[2], (OFF, NB), 0, 8) < 7).astype(jnp.int32), jax.random.fold_in(key_of[2], 1), 0, 1)
    dilation = draw_dilation(jax.random.fold_in(key_of[7], 71), 0)
    w_first = noise(key_of[4], (C, 9, C), (9 * C) ** -0.5, 0.375)
    b_first = noise(key_of[5], (C,), 0.5, 3.0, (), jnp.float32)
    w_second = noise(key_of[6], (C, 9, C), (9 * C) ** -0.5, 0.375)
    return {"features": features, "cotangent": cotangent, "band_mask": band_mask, "dilation": dilation, "w_first": w_first, "b_first": b_first, "w_second": w_second}


def dsilu(values):
    squash = jax.nn.sigmoid(values)
    return squash * (1.0 + values * (1.0 - squash))

def patch_block(padded, rate_value, flip_sign, first_bin, width_bins):
    pieces = []
    for a_off in (-1, 0, 1):
        for b_off in (-1, 0, 1):
            d_start = (2 * RMAX + flip_sign * (b_off - a_off) * rate_value).astype(jnp.int32)
            i_start = (RMAX + flip_sign * a_off * rate_value + first_bin).astype(jnp.int32)
            pieces.append(lax.dynamic_slice(padded, (jnp.int32(0), d_start, i_start), (C, OFF, width_bins)))
    return jnp.concatenate(pieces, axis=0)

def pad_field(field_in):
    return jnp.pad(field_in, ((0, 0), (2 * RMAX, 2 * RMAX), (RMAX, RMAX)))

def conv_full(field_in, matrix, rate_value, flip_sign):
    padded = pad_field(field_in)
    block_count = NB // BIN_DEV

    def one_block(block_index):
        patches = patch_block(padded, rate_value, flip_sign, block_index * BIN_DEV, BIN_DEV)
        return jnp.einsum('ok,kdi->odi', matrix.astype(jnp.float32), patches.astype(jnp.float32))
    blocks = lax.map(one_block, jnp.arange(block_count, dtype=jnp.int32))
    return jnp.transpose(blocks, (1, 2, 0, 3)).reshape(C, OFF, NB)

def weight_grad(field_in, upstream, rate_value):
    padded = pad_field(field_in)
    block_count = NB // BIN_DEV

    def one_block(block_index):
        patches = patch_block(padded, rate_value, 1, block_index * BIN_DEV, BIN_DEV)
        upstream_part = lax.dynamic_slice(upstream, (jnp.int32(0), jnp.int32(0), (block_index * BIN_DEV).astype(jnp.int32)), (C, OFF, BIN_DEV))
        return jnp.einsum('odi,kdi->ok', upstream_part.astype(jnp.float32), patches.astype(jnp.float32))
    return lax.optimization_barrier(jnp.sum(lax.map(one_block, jnp.arange(block_count, dtype=jnp.int32)), axis=0))

def reference(features, cotangent, band_mask, dilation, w_first, b_first, w_second):
    mask_float = band_mask.astype(jnp.float32)[None]
    rate_one = dilation[0]
    rate_two = dilation[1]
    matrix_one = w_first.reshape(C, 9 * C)
    matrix_two = w_second.reshape(C, 9 * C)
    trans_one = jnp.transpose(w_first, (2, 1, 0)).reshape(C, 9 * C)
    trans_two = jnp.transpose(w_second, (2, 1, 0)).reshape(C, 9 * C)
    feat_full = features.astype(jnp.float32)
    act_in = (jax.nn.silu(feat_full) * mask_float).astype(jnp.bfloat16)
    pre_act = conv_full(act_in, matrix_one, rate_one, 1) + b_first.astype(jnp.float32)[:, None, None]
    hidden = (jax.nn.silu(pre_act) * mask_float).astype(jnp.bfloat16)
    branch = conv_full(hidden, matrix_two, rate_two, 1)
    output = (feat_full + mask_float * branch).astype(jnp.bfloat16)
    upstream = cotangent.astype(jnp.float32)
    grad_out = (upstream * mask_float).astype(jnp.bfloat16)
    factor = 1.0 / jnp.sqrt(jnp.float32(CELLS))
    grad_two = weight_grad(hidden, grad_out, rate_two) * factor
    grad_hid = conv_full(grad_out, trans_two, rate_two, -1)
    grad_pre = (grad_hid * mask_float * dsilu(pre_act)).astype(jnp.bfloat16)
    grad_one = weight_grad(act_in, grad_pre, rate_one) * factor
    grad_bias = lax.optimization_barrier(jnp.sum(grad_pre.astype(jnp.float32), axis=(1, 2))) * factor
    grad_act = conv_full(grad_pre, trans_one, rate_one, -1)
    grad_features = (upstream + mask_float * dsilu(feat_full) * grad_act).astype(jnp.bfloat16)
    return (output, grad_features, grad_one.reshape(C, 9, C), grad_bias, grad_two.reshape(C, 9, C))
```

```python
import jax
import jax.numpy as jnp
from jax import lax
from jax.experimental import pallas as pl
from jax.experimental.pallas import tpu as pltpu
from jax.sharding import PartitionSpec as P

OFF = 192
RMAX = 8


def with_halo(shard, sides, width):
    for axis, dim in sides:
        size, length = (lax.axis_size(axis), shard.shape[dim])
        up = [(i, (i + 1) % size) for i in range(size - 1)]
        down = [(j, i) for i, j in up]
        last = lax.slice_in_dim(shard, length - width, length, axis=dim)
        initial = lax.slice_in_dim(shard, 0, width, axis=dim)
        before = lax.ppermute(last, axis, up)
        after = lax.ppermute(initial, axis, down)
        shard = jnp.concatenate([before, shard, after], axis=dim)
    return shard


def dsilu(values):
    squash = jax.nn.sigmoid(values)
    return squash * (1.0 + values * (1.0 - squash))


def extend(field_in):
    wider = with_halo(field_in, (("diag", 1),), 2 * RMAX)
    return with_halo(wider, (("bins", 2),), RMAX)


def local_patches(padded, rate_value, flip_sign, offsets, columns):
    pieces = []
    for a_off in (-1, 0, 1):
        for b_off in (-1, 0, 1):
            d_start = 2 * RMAX + flip_sign * (b_off - a_off) * rate_value
            i_start = RMAX + flip_sign * a_off * rate_value
            pieces.append(
                lax.dynamic_slice(
                    padded, (jnp.int32(0), d_start, i_start), (padded.shape[0], offsets, columns)
                )
            )
    return jnp.concatenate(pieces, axis=0)


def apply_taps(matrix, patches):
    return jnp.einsum("ok,kdi->odi", matrix, patches, preferred_element_type=jnp.float32)


def tap_sums(upstream, patches):
    return jnp.einsum("odi,kdi->ok", upstream, patches, preferred_element_type=jnp.float32)


def shards(features, cotangent, band_mask, dilation, w_first, b_first, w_second):
    channels, offsets, columns = features.shape
    mask_float = band_mask.astype(jnp.float32)[None]
    rate_one = dilation[0]
    rate_two = dilation[1]
    matrix_one = w_first.reshape(channels, 9 * channels)
    matrix_two = w_second.reshape(channels, 9 * channels)
    trans_one = jnp.transpose(w_first, (2, 1, 0)).reshape(channels, 9 * channels)
    trans_two = jnp.transpose(w_second, (2, 1, 0)).reshape(channels, 9 * channels)
    factor = 1.0 / jnp.sqrt(jnp.float32(OFF) * jnp.float32(columns * lax.axis_size("bins")))
    feat_full = features.astype(jnp.float32)
    upstream = cotangent.astype(jnp.float32)
    act_in = (jax.nn.silu(feat_full) * mask_float).astype(jnp.bfloat16)
    patches_one = local_patches(extend(act_in), rate_one, 1, offsets, columns)
    pre_act = apply_taps(matrix_one, patches_one) + b_first[:, None, None]
    hidden = (jax.nn.silu(pre_act) * mask_float).astype(jnp.bfloat16)
    patches_two = local_patches(extend(hidden), rate_two, 1, offsets, columns)
    output = (feat_full + mask_float * apply_taps(matrix_two, patches_two)).astype(jnp.bfloat16)
    grad_out = (upstream * mask_float).astype(jnp.bfloat16)
    local_two = tap_sums(grad_out, patches_two)
    grad_hid = apply_taps(
        trans_two, local_patches(extend(grad_out), rate_two, -1, offsets, columns)
    )
    grad_pre = (grad_hid * mask_float * dsilu(pre_act)).astype(jnp.bfloat16)
    grad_act = apply_taps(
        trans_one, local_patches(extend(grad_pre), rate_one, -1, offsets, columns)
    )
    local_one = tap_sums(grad_pre, patches_one)
    local_bias = jnp.sum(grad_pre.astype(jnp.float32), axis=(1, 2))
    grad_features = (upstream + mask_float * dsilu(feat_full) * grad_act).astype(jnp.bfloat16)
    flat = jnp.concatenate([local_one.reshape(-1), local_two.reshape(-1), local_bias])
    count = channels * 9 * channels
    rows = -(-flat.shape[0] // (GROUP * 128))
    flat = jnp.pad(flat, (0, GROUP * rows * 128 - flat.shape[0]))
    summed = sum_everywhere(flat.reshape(GROUP, rows, 128)).reshape(-1)
    total_one, total_two = summed[:count], summed[count : 2 * count]
    total_bias = summed[2 * count : 2 * count + channels]
    grad_one = (total_one * factor).reshape(channels, 9, channels)
    grad_two = (total_two * factor).reshape(channels, 9, channels)
    return (output, grad_features, grad_one, total_bias * factor, grad_two)


NEAR = 8
GROUP = 16
MESH = pl.DeviceIdType.MESH


def ring_sum_kernel(x_ref, out_ref, got, part, send1, recv1, send2, recv2, send3, recv3):
    bins, diag = lax.axis_index("bins"), lax.axis_index("diag")
    near, far = (bins % NEAR) * 2 + diag, bins // NEAR

    def near_peer(step):
        rank = (near + step) % GROUP
        return rank, (far * NEAR + rank // 2, rank % 2)

    def far_peer(step):
        rank = (far + step) % GROUP
        return rank, (rank * NEAR + bins % NEAR, diag)

    barrier = pltpu.get_barrier_semaphore()
    for step in range(1, GROUP):
        pl.semaphore_signal(barrier, inc=1, device_id=near_peer(step)[1], device_id_type=MESH)
        pl.semaphore_signal(barrier, inc=1, device_id=far_peer(step)[1], device_id_type=MESH)
    pl.semaphore_wait(barrier, 2 * (GROUP - 1))

    copies = []
    for step in range(1, GROUP):
        rank, device = near_peer(step)
        copy = pltpu.make_async_remote_copy(
            src_ref=x_ref.at[rank], dst_ref=got.at[step], send_sem=send1.at[step],
            recv_sem=recv1.at[step], device_id=device, device_id_type=MESH)
        copy.start()
        copies.append(copy)
    total = x_ref[near]
    for step in range(1, GROUP):
        copies[step - 1].wait_recv()
        total = total + got[step]
    part[far] = total
    spread = []
    for step in range(1, GROUP):
        rank, device = far_peer(step)
        copy = pltpu.make_async_remote_copy(
            src_ref=part.at[far], dst_ref=part.at[far], send_sem=send2.at[step],
            recv_sem=recv2.at[step], device_id=device, device_id_type=MESH)
        copy.start()
        spread.append(copy)
    for copy in copies:
        copy.wait_send()
    for copy in spread:
        copy.wait_recv()
    total = part[0]
    for rank in range(1, GROUP):
        total = total + part[rank]
    out_ref[near] = total
    gather = []
    for step in range(1, GROUP):
        rank, device = near_peer(step)
        copy = pltpu.make_async_remote_copy(
            src_ref=out_ref.at[near], dst_ref=out_ref.at[near], send_sem=send3.at[step],
            recv_sem=recv3.at[step], device_id=device, device_id_type=MESH)
        copy.start()
        gather.append(copy)
    for copy in spread:
        copy.wait_send()
    for copy in gather:
        copy.wait()


def sum_everywhere(values):
    rows = values.shape[1]
    sems = [pltpu.SemaphoreType.DMA((GROUP,)) for _ in range(6)]
    return pl.pallas_call(
        ring_sum_kernel,
        out_shape=jax.ShapeDtypeStruct(values.shape, jnp.float32),
        in_specs=[pl.BlockSpec(memory_space=pltpu.VMEM)],
        out_specs=pl.BlockSpec(memory_space=pltpu.VMEM),
        scratch_shapes=[
            pltpu.VMEM((GROUP, rows, 128), jnp.float32),
            pltpu.VMEM((GROUP, rows, 128), jnp.float32),
        ] + sems,
        compiler_params=pltpu.CompilerParams(collective_id=0, has_side_effects=True),
    )(values)


def solution(mesh):
    in_specs = (
        P(None, "diag", "bins"),
        P(None, "diag", "bins"),
        P("diag", "bins"),
        P(),
        P(),
        P(),
        P(),
    )
    out_specs = (P(None, "diag", "bins"), P(None, "diag", "bins"), P(), P(), P())
    return jax.shard_map(shards, mesh=mesh, in_specs=in_specs, out_specs=out_specs, check_vma=False)
```

```python
import jax
import jax.numpy as jnp
from jax import lax
from jax.experimental import pallas as pl
from jax.experimental.pallas import tpu as pltpu
from jax.sharding import PartitionSpec as P

F32, BF16 = jnp.float32, jnp.bfloat16
MESH = pl.DeviceIdType.MESH
C = 32
ROWS = 96
LANES = 128
HALO = 16
STRIP = 8
EXT = ROWS + 2 * HALO
CHUNKS = ROWS // HALO
NEAR = 8
GROUP = 16
PARTS = 10
CELLS = 3145728
TAPS = [(a, b) for a in (-1, 0, 1) for b in (-1, 0, 1)]
STEP = 4


def sigmoid(v):
    return 1.0 / (1.0 + jnp.exp(-v))


def kernel(
    rate, feat, cot, mask, w1, b1, w2,
    out, gfeat, g1, gb, g2,
    own, strips, shifted, maskf, slope, weights, wstage, bias, conv,
    got_d, got_i, got_c, sums, got, part, total,
    send_d, recv_d, send_i, recv_i, send_c, recv_c, send1, recv1, send2, recv2, send3, recv3,
):
    bins, diag = lax.axis_index("bins"), lax.axis_index("diag")
    count = lax.axis_size("bins")
    right, left = (bins + 1) % count, (bins + count - 1) % count
    across = 1 - diag
    near, far = (bins % NEAR) * 2 + diag, bins // NEAR

    def near_peer(step):
        rank = (near + step) % GROUP
        return rank, (far * NEAR + rank // 2, rank % 2)

    def far_peer(step):
        rank = (far + step) % GROUP
        return rank, (rank * NEAR + bins % NEAR, diag)

    peers = [near_peer(s)[1] for s in range(1, GROUP)] + [far_peer(s)[1] for s in range(1, GROUP)]
    peers += [(left, diag), (right, diag), (left, across), (right, across)]
    barrier = pltpu.get_barrier_semaphore()
    for peer in peers:
        pl.semaphore_signal(barrier, inc=1, device_id=peer, device_id_type=MESH)

    r1, r2 = rate[0], rate[1]
    lane = lax.broadcasted_iota(jnp.int32, (C, LANES), 1)
    edge_start = (ROWS - HALO) * (1 - diag)
    edge_chunk = (CHUNKS - 1) * (1 - diag)
    halo_start = (ROWS + HALO) * (1 - diag)
    zero_start = (ROWS + HALO) * diag

    maskf[...] = mask[...].astype(F32)

    def enter(q, _):
        rows = pl.ds(pl.multiple_of(q * HALO, HALO), HALO)
        m = maskf[rows, :][None]
        x = feat[:, rows, :].astype(F32)
        s = sigmoid(x)
        act = (x * s * m).astype(BF16)
        slope[:, rows, :] = m * s * (1.0 + x * (1.0 - s))
        own[0, rows] = jnp.transpose(act, (1, 0, 2))
        grad = (cot[:, rows, :].astype(F32) * m).astype(BF16)
        own[1, rows] = jnp.transpose(grad, (1, 0, 2))
        return 0

    lax.fori_loop(0, CHUNKS, enter, 0)

    def pack(field):
        def chunk(q, _):
            up = jnp.zeros((C, LANES), BF16)
            down = jnp.zeros((C, LANES), BF16)
            for j in range(HALO):
                row = own[field, q * HALO + j]
                inside = (lane >= STRIP * j) & (lane < STRIP * (j + 1))
                up = jnp.where(inside, pltpu.roll(row, (STRIP * (j + 1)) % LANES, 1), up)
                down = jnp.where(inside, pltpu.roll(row, STRIP * j, 1), down)
            strips[0, field, q] = up
            strips[1, field, q] = down
            return 0

        lax.fori_loop(0, CHUNKS, chunk, 0)

    def exchange(rnd):
        two = pl.ds(2 * rnd, 2)
        copies = [
            pltpu.make_async_remote_copy(
                src_ref=own.at[two, pl.ds(edge_start, HALO)], dst_ref=got_d.at[rnd],
                send_sem=send_d.at[rnd], recv_sem=recv_d.at[rnd],
                device_id=(bins, across), device_id_type=MESH)
        ]
        for side, to in enumerate((right, left)):
            copies.append(
                pltpu.make_async_remote_copy(
                    src_ref=strips.at[side, two], dst_ref=got_i.at[rnd, side],
                    send_sem=send_i.at[rnd, side], recv_sem=recv_i.at[rnd, side],
                    device_id=(to, diag), device_id_type=MESH))
            copies.append(
                pltpu.make_async_remote_copy(
                    src_ref=strips.at[side, two, edge_chunk], dst_ref=got_c.at[rnd, side],
                    send_sem=send_c.at[rnd, side], recv_sem=recv_c.at[rnd, side],
                    device_id=(to, across), device_id_type=MESH))
        return copies

    def clear_ends(rnd):
        for side, end in ((0, 0), (1, count - 1)):
            @pl.when(bins == end)
            def _():
                got_i[rnd, side] = jnp.zeros(got_i.shape[2:], BF16)
                got_c[rnd, side] = jnp.zeros(got_c.shape[2:], BF16)

    def shift_rows(row_of, before, after, r, store):
        for j in range(HALO):
            row = row_of(j)
            low = pltpu.roll(before, (r - STRIP * (j + 1) + LANES) % LANES, 1)
            high = pltpu.roll(after, (2 * LANES - r - STRIP * j) % LANES, 1)
            store(j, 0, jnp.where(lane < r, low, pltpu.roll(row, r, 1)))
            store(j, 1, row)
            store(j, 2, jnp.where(lane >= LANES - r, high, pltpu.roll(row, LANES - r, 1)))

    def shift(field, r):
        rnd, slot = field // 2, field % 2

        def chunk(q, _):
            def store(j, a, value):
                shifted[field, a, HALO + q * HALO + j] = value

            shift_rows(lambda j: own[field, q * HALO + j], got_i[rnd, 0, slot, q],
                       got_i[rnd, 1, slot, q], r, store)
            return 0

        lax.fori_loop(0, CHUNKS, chunk, 0)

        def store(j, a, value):
            shifted[field, a, halo_start + j] = value

        shift_rows(lambda j: got_d[rnd, slot, j], got_c[rnd, 0, slot], got_c[rnd, 1, slot], r, store)
        for a in range(3):
            shifted[field, a, pl.ds(zero_start, HALO)] = jnp.zeros((HALO, C, LANES), BF16)

    def patches(field, r, sign, d, step):
        blocks = []
        for a, b in TAPS:
            start = HALO + d + sign * (b - a) * r
            blocks.append(
                jnp.concatenate([shifted[field, sign * a + 1, start + j] for j in range(step)], axis=1)
            )
        return jnp.concatenate(blocks, axis=0)

    pack(0)
    pack(1)
    pl.semaphore_wait(barrier, len(peers))
    first = exchange(0)
    for copy in first:
        copy.start()

    bias[...] = jnp.broadcast_to(jnp.transpose(jnp.broadcast_to(b1[...], (C, C)))[:, :1], (C, LANES))
    for k, ref in enumerate((w1, w2)):
        wstage[...] = ref[...].astype(F32)
        taps = [wstage[:, t, :] for t in range(9)]
        weights[2 * k] = jnp.concatenate(taps, axis=1).astype(BF16)
        weights[2 * k + 1] = jnp.concatenate([jnp.transpose(t) for t in taps], axis=1).astype(BF16)

    for copy in first:
        copy.wait()
    clear_ends(0)
    shift(0, r1)
    shift(1, r2)

    def middle(n, _):
        d = n * STEP
        pre = jnp.dot(weights[0], patches(0, r1, 1, d, STEP), preferred_element_type=F32)
        back = jnp.dot(weights[3], patches(1, r2, -1, d, STEP), preferred_element_type=F32)
        for j in range(STEP):
            m = maskf[pl.ds(d + j, 1), :]
            y = pre[:, j * LANES : (j + 1) * LANES] + bias[...]
            s = sigmoid(y)
            own[2, d + j] = (y * s * m).astype(BF16)
            grad = back[:, j * LANES : (j + 1) * LANES] * m * (s * (1.0 + y * (1.0 - s)))
            own[3, d + j] = grad.astype(BF16)
        return 0

    lax.fori_loop(0, ROWS // STEP, middle, 0, unroll=2)

    pack(2)
    pack(3)
    second = exchange(1)
    for copy in second:
        copy.start()

    wide = 16

    def grads(n, carry):
        d = n * wide
        upstream = jnp.concatenate([own[3, d + j] for j in range(wide)], axis=1)
        hidden = jnp.concatenate([own[2, d + j] for j in range(wide)], axis=1)
        nt = (((1,), (1,)), ((), ()))
        one = lax.dot_general(patches(0, r1, 1, d, wide), upstream, nt, preferred_element_type=F32)
        two = lax.dot_general(patches(1, r2, -1, d, wide), hidden, nt, preferred_element_type=F32)
        ones = jnp.ones((16, wide * LANES), BF16)
        total_b = lax.dot_general(ones, upstream, nt, preferred_element_type=F32)
        return carry[0] + one, carry[1] + two, carry[2] + total_b

    zero = jnp.zeros((9 * C, C), F32)
    one, two, bias_sum = lax.fori_loop(0, ROWS // wide, grads, (zero, zero, jnp.zeros((16, C), F32)))
    for k, value in enumerate((one, two)):
        wide4 = jnp.concatenate([value[2 * C * g : 2 * C * (g + 1)] for g in range(4)], axis=1)
        for p in range(4):
            sums[4 * k + p] = wide4[HALO * p : HALO * (p + 1)]
    last = [one[8 * C :], two[8 * C :], jnp.concatenate([bias_sum, jnp.zeros((16, C), F32)], axis=0)]
    last = jnp.concatenate(last + [jnp.zeros((C, C), F32)], axis=1)
    sums[8] = last[:HALO]
    sums[9] = last[HALO:]

    def scatter(step):
        rank, device = near_peer(step)
        return rank, pltpu.make_async_remote_copy(
            src_ref=sums.at[rank % PARTS], dst_ref=got.at[step], send_sem=send1.at[step],
            recv_sem=recv1.at[step], device_id=device, device_id_type=MESH)

    for step in range(1, GROUP):
        rank, copy = scatter(step)
        pl.when(rank < PARTS)(copy.start)

    for copy in second:
        copy.wait()
    clear_ends(1)
    shift(2, r2)

    def forward(n, _):
        d = n * STEP
        y = jnp.dot(weights[2], patches(2, r2, 1, d, STEP), preferred_element_type=F32)
        for j in range(STEP):
            conv[d + j] = y[:, j * LANES : (j + 1) * LANES]
        return 0

    lax.fori_loop(0, ROWS // STEP, forward, 0, unroll=2)

    def finish_forward(q, _):
        rows = pl.ds(pl.multiple_of(q * HALO, HALO), HALO)
        y = jnp.transpose(conv[rows], (1, 0, 2))
        out[:, rows, :] = (feat[:, rows, :].astype(F32) + maskf[rows, :][None] * y).astype(BF16)
        return 0

    lax.fori_loop(0, CHUNKS, finish_forward, 0)

    for step in range(1, GROUP):
        rank, copy = scatter(step)
        pl.when(rank < PARTS)(copy.wait_send)

    spread = []
    for step in range(1, GROUP):
        rank, device = far_peer(step)
        spread.append(pltpu.make_async_remote_copy(
            src_ref=part.at[far], dst_ref=part.at[far], send_sem=send2.at[step],
            recv_sem=recv2.at[step], device_id=device, device_id_type=MESH))

    @pl.when(near < PARTS)
    def _():
        value = sums[near % PARTS]
        for step in range(1, GROUP):
            scatter(step)[1].wait_recv()
            value = value + got[step]
        part[far] = value
        for copy in spread:
            copy.start()

    shift(3, r1)

    def backward(n, _):
        d = n * STEP
        y = jnp.dot(weights[1], patches(3, r1, -1, d, STEP), preferred_element_type=F32)
        for j in range(STEP):
            conv[d + j] = y[:, j * LANES : (j + 1) * LANES]
        return 0

    lax.fori_loop(0, ROWS // STEP, backward, 0, unroll=2)

    def finish_backward(q, _):
        rows = pl.ds(pl.multiple_of(q * HALO, HALO), HALO)
        y = jnp.transpose(conv[rows], (1, 0, 2))
        gfeat[:, rows, :] = (cot[:, rows, :].astype(F32) + slope[:, rows, :] * y).astype(BF16)
        return 0

    lax.fori_loop(0, CHUNKS, finish_backward, 0)

    def gather(step):
        return near_peer(step)[0], pltpu.make_async_remote_copy(
            src_ref=total.at[near % PARTS], dst_ref=total.at[near % PARTS], send_sem=send3.at[step],
            recv_sem=recv3.at[step], device_id=near_peer(step)[1], device_id_type=MESH)

    @pl.when(near < PARTS)
    def _():
        for copy in spread:
            copy.wait_recv()
        value = part[0]
        for rank in range(1, GROUP):
            value = value + part[rank]
        total[near % PARTS] = value
        for step in range(1, GROUP):
            gather(step)[1].start()
        for copy in spread:
            copy.wait_send()
        for step in range(1, GROUP):
            gather(step)[1].wait_send()

    for step in range(1, GROUP):
        sender = (near - step + GROUP) % GROUP
        pl.when(sender < PARTS)(gather(step)[1].wait_recv)

    factor = 1.0 / jnp.sqrt(jnp.float32(CELLS))
    last = jnp.concatenate([total[8], total[9]], axis=0) * factor
    for k, ref in enumerate((g1, g2)):
        body = jnp.concatenate([total[4 * k + p] for p in range(4)], axis=0) * factor
        for t in range(9):
            if t < 8:
                block = body[(t % 2) * C : (t % 2 + 1) * C, (t // 2) * C : (t // 2 + 1) * C]
            else:
                block = last[:, k * C : (k + 1) * C]
            ref[:, t, :] = jnp.transpose(block) if k == 0 else block
    gb[...] = last[:1, 2 * C : 3 * C]


def shards(features, cotangent, band_mask, dilation, w_first, b_first, w_second):
    vmem = pl.BlockSpec(memory_space=pltpu.VMEM)
    dma = pltpu.SemaphoreType.DMA
    shape = jax.ShapeDtypeStruct
    field = (C, ROWS, LANES)
    taps = (C, 9, C)
    out, gfeat, g1, gb, g2 = pl.pallas_call(
        kernel,
        out_shape=[shape(field, BF16), shape(field, BF16), shape(taps, F32), shape((1, C), F32), shape(taps, F32)],
        in_specs=[pl.BlockSpec(memory_space=pltpu.SMEM)] + [vmem] * 6,
        out_specs=[vmem] * 5,
        scratch_shapes=[
            pltpu.VMEM((4, ROWS, C, LANES), BF16),
            pltpu.VMEM((2, 4, CHUNKS, C, LANES), BF16),
            pltpu.VMEM((4, 3, EXT, C, LANES), BF16),
            pltpu.VMEM((ROWS, LANES), F32),
            pltpu.VMEM(field, F32),
            pltpu.VMEM((4, C, 9 * C), BF16),
            pltpu.VMEM(taps, F32),
            pltpu.VMEM((C, LANES), F32),
            pltpu.VMEM((ROWS, C, LANES), F32),
            pltpu.VMEM((2, 2, HALO, C, LANES), BF16),
            pltpu.VMEM((2, 2, 2, CHUNKS, C, LANES), BF16),
            pltpu.VMEM((2, 2, 2, C, LANES), BF16),
            pltpu.VMEM((PARTS, HALO, LANES), F32),
            pltpu.VMEM((GROUP, HALO, LANES), F32),
            pltpu.VMEM((GROUP, HALO, LANES), F32),
            pltpu.VMEM((PARTS, HALO, LANES), F32),
            dma((2,)), dma((2,)), dma((2, 2)), dma((2, 2)), dma((2, 2)), dma((2, 2)),
            dma((GROUP,)), dma((GROUP,)), dma((GROUP,)), dma((GROUP,)), dma((GROUP,)), dma((GROUP,)),
        ],
        compiler_params=pltpu.CompilerParams(
            collective_id=0, has_side_effects=True, vmem_limit_bytes=48 * 1024 * 1024
        ),
    )(dilation, features, cotangent, band_mask, w_first, b_first[None], w_second)
    return (out, gfeat, g1, gb[0], g2)


def solution(mesh):
    field, whole = P(None, "diag", "bins"), P()
    return jax.shard_map(
        shards, mesh=mesh, in_specs=(field, field, P("diag", "bins"), whole, whole, whole, whole),
        out_specs=(field, field, whole, whole, whole), check_vma=False)
```

```python
import jax
import jax.numpy as jnp
from jax import lax
from jax.experimental import pallas as pl
from jax.experimental.pallas import tpu as pltpu
from jax.sharding import PartitionSpec as P

F32, BF16 = jnp.float32, jnp.bfloat16
MESH = pl.DeviceIdType.MESH
C = 32
ROWS = 96
LANES = 128
HALO = 16
STRIP = 8
EXT = ROWS + 2 * HALO
CHUNKS = ROWS // HALO
NEAR = 8
GROUP = 16
PARTS = 10
CELLS = 3145728
PAD = 2 * HALO
LAGS = (-2, -1, 0, 1, 2)
TAPS = [(a, b) for a in (-1, 0, 1) for b in (-1, 0, 1)]
STEP = 4


def sigmoid(v):
    return 0.5 + 0.5 * jnp.tanh(0.5 * v)


def kernel(
    rate, feat_in, cot_in, mask_in, w1_in, b1_in, w2_in,
    out_hbm, gfeat_hbm, g1, gb, g2,
    out, gfeat, feat, cot, mask, w1, b1, w2, own, padded, strips, shifted, maskf, weights, bias, conv,
    got_d, got_i, got_c, sums, got, part, total, load,
    send_d, recv_d, send_i, recv_i, send_c, recv_c, send1, recv1, send2, recv2, send3, recv3,
):
    bins, diag = lax.axis_index("bins"), lax.axis_index("diag")
    count = lax.axis_size("bins")
    right, left = (bins + 1) % count, (bins + count - 1) % count
    across = 1 - diag
    near, far = (bins % NEAR) * 2 + diag, bins // NEAR

    def near_peer(step):
        rank = (near + step) % GROUP
        return rank, (far * NEAR + rank // 2, rank % 2)

    def far_peer(step):
        rank = (far + step) % GROUP
        return rank, (rank * NEAR + bins % NEAR, diag)

    peers = [near_peer(s)[1] for s in range(1, GROUP)] + [far_peer(s)[1] for s in range(1, GROUP)]
    peers += [(left, diag), (right, diag), (left, across), (right, across)]
    barrier = pltpu.get_barrier_semaphore()
    for peer in peers:
        pl.semaphore_signal(barrier, inc=1, device_id=peer, device_id_type=MESH)

    r1, r2 = rate[0], rate[1]
    lane = lax.broadcasted_iota(jnp.int32, (C, LANES), 1)
    edge_start = (ROWS - HALO) * (1 - diag)
    edge_chunk = (CHUNKS - 1) * (1 - diag)
    halo_start = (ROWS + HALO) * (1 - diag)
    zero_start = (ROWS + HALO) * diag

    edge = pl.ds(pl.multiple_of(edge_start, HALO), HALO)
    rest = pl.ds(pl.multiple_of(HALO * diag, HALO), ROWS - HALO)
    loads = [
        pltpu.make_async_copy(src, dst, load.at[k])
        for k, (src, dst) in enumerate((
            (mask_in, mask),
            (feat_in.at[:, edge], feat.at[:, edge]),
            (cot_in.at[:, edge], cot.at[:, edge]),
            (feat_in.at[:, rest], feat.at[:, rest]),
            (cot_in.at[:, rest], cot.at[:, rest]),
            (w1_in, w1),
            (w2_in, w2),
            (b1_in, b1),
        ))
    ]
    for copy in loads:
        copy.start()
    for field in (0, 1):
        padded[field, :PAD] = jnp.zeros((PAD, C, LANES), BF16)
        padded[field, PAD + ROWS :] = jnp.zeros((PAD, C, LANES), BF16)
    for field in range(4):
        for a in range(3):
            shifted[field, a, pl.ds(zero_start, HALO)] = jnp.zeros((HALO, C, LANES), BF16)
    loads[0].wait()
    maskf[...] = mask[...].astype(F32)

    def enter(q):
        rows = pl.ds(pl.multiple_of(q * HALO, HALO), HALO)
        m = maskf[rows, :][None]
        x = feat[:, rows, :].astype(F32)
        own[0, rows] = jnp.transpose((x * sigmoid(x) * m).astype(BF16), (1, 0, 2))
        grad = (cot[:, rows, :].astype(F32) * m).astype(BF16)
        own[1, rows] = jnp.transpose(grad, (1, 0, 2))

    def pack(field):
        def chunk(q, _):
            up = jnp.zeros((C, LANES), BF16)
            down = jnp.zeros((C, LANES), BF16)
            for j in range(HALO):
                row = row_of(field, q * HALO + j)
                inside = (lane >= STRIP * j) & (lane < STRIP * (j + 1))
                up = jnp.where(inside, pltpu.roll(row, (STRIP * (j + 1)) % LANES, 1), up)
                down = jnp.where(inside, pltpu.roll(row, STRIP * j, 1), down)
            strips[0, field, q] = up
            strips[1, field, q] = down
            return 0

        lax.fori_loop(0, CHUNKS, chunk, 0)

    def edges(rnd, src):
        return pltpu.make_async_remote_copy(
            src_ref=src, dst_ref=got_d.at[rnd], send_sem=send_d.at[rnd], recv_sem=recv_d.at[rnd],
            device_id=(bins, across), device_id_type=MESH)

    def sides(field):
        copies = []
        for side, to in enumerate((right, left)):
            copies.append(
                pltpu.make_async_remote_copy(
                    src_ref=strips.at[side, field], dst_ref=got_i.at[side, field],
                    send_sem=send_i.at[side, field], recv_sem=recv_i.at[side, field],
                    device_id=(to, diag), device_id_type=MESH))
            copies.append(
                pltpu.make_async_remote_copy(
                    src_ref=strips.at[side, field, edge_chunk], dst_ref=got_c.at[side, field],
                    send_sem=send_c.at[side, field], recv_sem=recv_c.at[side, field],
                    device_id=(to, across), device_id_type=MESH))
        return copies

    def clear_ends(field):
        for side, end in ((0, 0), (1, count - 1)):
            @pl.when(bins == end)
            def _():
                got_i[side, field] = jnp.zeros(got_i.shape[2:], BF16)
                got_c[side, field] = jnp.zeros(got_c.shape[2:], BF16)

    def shift_rows(row_of, before, after, r, store):
        for j in range(HALO):
            row = row_of(j)
            low = pltpu.roll(before, (r - STRIP * (j + 1) + LANES) % LANES, 1)
            high = pltpu.roll(after, (2 * LANES - r - STRIP * j) % LANES, 1)
            store(j, 0, jnp.where(lane < r, low, pltpu.roll(row, r, 1)))
            store(j, 1, row)
            store(j, 2, jnp.where(lane >= LANES - r, high, pltpu.roll(row, LANES - r, 1)))

    def row_of(field, d):
        return own[field, d] if field < 2 else padded[field - 2, PAD + d]

    def shift(field, r):
        def chunk(q, _):
            def store(j, a, value):
                shifted[field, a, HALO + q * HALO + j] = value

            shift_rows(lambda j: row_of(field, q * HALO + j), got_i[0, field, q], got_i[1, field, q], r, store)
            return 0

        lax.fori_loop(0, CHUNKS, chunk, 0)

    def shift_halo(field, r):
        def store(j, a, value):
            shifted[field, a, halo_start + j] = value

        rows = got_d.at[field // 2, field % 2]
        shift_rows(lambda j: rows[j], got_c[0, field], got_c[1, field], r, store)

    def patches(field, r, sign, d, step):
        blocks = []
        for a, b in TAPS:
            start = HALO + d + sign * (b - a) * r
            blocks.append(
                jnp.concatenate([shifted[field, sign * a + 1, start + j] for j in range(step)], axis=1)
            )
        return jnp.concatenate(blocks, axis=0)

    loads[1].wait()
    loads[2].wait()
    enter(edge_chunk)
    pl.semaphore_wait(barrier, len(peers))
    edge_one = edges(0, own.at[:, edge])
    edge_one.start()
    loads[3].wait()
    loads[4].wait()

    def enter_rest(n, _):
        enter(n + diag)
        return 0

    lax.fori_loop(0, CHUNKS - 1, enter_rest, 0)
    pack(0)
    strips_a = sides(0)
    for copy in strips_a:
        copy.start()
    pack(1)
    strips_g = sides(1)
    for copy in strips_g:
        copy.start()

    for copy in loads[5:]:
        copy.wait()
    bias[...] = jnp.broadcast_to(jnp.transpose(jnp.broadcast_to(b1[...], (C, C)))[:, :1], (C, LANES))
    for k, ref in enumerate((w1, w2)):
        taps = [ref[t] for t in range(9)]
        weights[2 * k] = jnp.concatenate(taps, axis=1)
        weights[2 * k + 1] = jnp.concatenate(
            [jnp.transpose(t.astype(F32)).astype(BF16) for t in taps], axis=1)

    for copy in strips_a:
        copy.wait()
    clear_ends(0)
    shift(0, r1)
    for copy in strips_g:
        copy.wait()
    clear_ends(1)
    shift(1, r2)
    edge_one.wait()
    shift_halo(0, r1)
    shift_halo(1, r2)

    def middle(d):
        pre = jnp.dot(weights[0], patches(0, r1, 1, d, STEP), preferred_element_type=F32)
        back = jnp.dot(weights[3], patches(1, r2, -1, d, STEP), preferred_element_type=F32)
        for j in range(STEP):
            m = maskf[pl.ds(d + j, 1), :]
            y = pre[:, j * LANES : (j + 1) * LANES] + bias[...]
            s = sigmoid(y)
            padded[0, PAD + d + j] = (y * s * m).astype(BF16)
            grad = back[:, j * LANES : (j + 1) * LANES] * m * (s * (1.0 + y * (1.0 - s)))
            padded[1, PAD + d + j] = grad.astype(BF16)

    def middle_edge(n, _):
        middle(edge_start + n * STEP)
        return 0

    def middle_rest(n, _):
        middle(HALO * diag + n * STEP)
        return 0

    lax.fori_loop(0, HALO // STEP, middle_edge, 0, unroll=2)
    edge_two = edges(1, padded.at[:, pl.ds(PAD + edge_start, HALO)])
    edge_two.start()
    lax.fori_loop(0, (ROWS - HALO) // STEP, middle_rest, 0, unroll=2)

    wide = 16
    nt = (((1,), (1,)), ((), ()))

    def row_block(rows):
        return jnp.concatenate(rows, axis=1)

    def grads(n, carry):
        k = n * wide
        act = [row_block([shifted[0, a, k + j] for j in range(wide)]) for a in range(3)]
        act.append(jnp.ones((C, wide * LANES), BF16))
        ups = [row_block([padded[1, HALO + k - m * r1 + j] for j in range(wide)]) for m in LAGS]
        one = lax.dot_general(jnp.concatenate(ups, axis=0), jnp.concatenate(act, axis=0), nt,
                              preferred_element_type=F32)
        grad = [row_block([shifted[1, a, k + j] for j in range(wide)]) for a in range(3)]
        hid = [row_block([padded[0, HALO + k + m * r2 + j] for j in range(wide)]) for m in LAGS]
        two = lax.dot_general(jnp.concatenate(grad, axis=0), jnp.concatenate(hid, axis=0), nt,
                              preferred_element_type=F32)
        return carry[0] + one, carry[1] + two

    zero = (jnp.zeros((5 * C, 4 * C), F32), jnp.zeros((3 * C, 5 * C), F32))
    one, two = lax.fori_loop(0, EXT // wide, grads, zero)

    def block(value, i, j):
        return value[C * i : C * (i + 1), C * j : C * (j + 1)]

    blocks = [[block(one, b - a + 2, a + 1) for a, b in TAPS], [block(two, 1 - a, b - a + 2) for a, b in TAPS]]
    for k in range(2):
        for p in range(2):
            four = jnp.concatenate(blocks[k][4 * p : 4 * p + 4], axis=1)
            sums[4 * k + 2 * p] = four[:HALO]
            sums[4 * k + 2 * p + 1] = four[HALO:]
    four = jnp.concatenate([blocks[0][8], blocks[1][8], block(one, 2, 3), jnp.zeros((C, C), F32)], axis=1)
    sums[8] = four[:HALO]
    sums[9] = four[HALO:]

    def scatter(step):
        rank, device = near_peer(step)
        return rank, pltpu.make_async_remote_copy(
            src_ref=sums.at[rank % PARTS], dst_ref=got.at[step], send_sem=send1.at[step],
            recv_sem=recv1.at[step], device_id=device, device_id_type=MESH)

    for step in range(1, GROUP):
        rank, copy = scatter(step)
        pl.when(rank < PARTS)(copy.start)

    pack(2)
    strips_h = sides(2)
    for copy in strips_h:
        copy.start()
    pack(3)
    strips_q = sides(3)
    for copy in strips_q:
        copy.start()
    for copy in strips_h:
        copy.wait()
    clear_ends(2)
    shift(2, r2)
    edge_two.wait()
    shift_halo(2, r2)

    spread = []
    for step in range(1, GROUP):
        rank, device = far_peer(step)
        spread.append(pltpu.make_async_remote_copy(
            src_ref=part.at[far], dst_ref=part.at[far], send_sem=send2.at[step],
            recv_sem=recv2.at[step], device_id=device, device_id_type=MESH))

    @pl.when(near < PARTS)
    def _():
        value = sums[near % PARTS]
        for step in range(1, GROUP):
            scatter(step)[1].wait_recv()
            value = value + got[step]
        part[far] = value
        for copy in spread:
            copy.start()

    def forward(n, _):
        d = n * STEP
        y = jnp.dot(weights[2], patches(2, r2, 1, d, STEP), preferred_element_type=F32)
        for j in range(STEP):
            conv[d + j] = y[:, j * LANES : (j + 1) * LANES]
        return 0

    lax.fori_loop(0, ROWS // STEP, forward, 0, unroll=2)

    def finish_forward(q, _):
        rows = pl.ds(pl.multiple_of(q * HALO, HALO), HALO)
        y = jnp.transpose(conv[rows], (1, 0, 2))
        out[:, rows, :] = (feat[:, rows, :].astype(F32) + maskf[rows, :][None] * y).astype(BF16)
        return 0

    lax.fori_loop(0, CHUNKS, finish_forward, 0)
    store_out = pltpu.make_async_copy(out, out_hbm, load.at[0])
    store_out.start()
    for copy in strips_q:
        copy.wait()
    clear_ends(3)
    shift(3, r1)
    shift_halo(3, r1)

    def gather(step):
        return near_peer(step)[0], pltpu.make_async_remote_copy(
            src_ref=total.at[near % PARTS], dst_ref=total.at[near % PARTS], send_sem=send3.at[step],
            recv_sem=recv3.at[step], device_id=near_peer(step)[1], device_id_type=MESH)

    @pl.when(near < PARTS)
    def _():
        for copy in spread:
            copy.wait_recv()
        value = part[0]
        for rank in range(1, GROUP):
            value = value + part[rank]
        total[near % PARTS] = value
        for step in range(1, GROUP):
            gather(step)[1].start()

    def backward(n, _):
        d = n * STEP
        y = jnp.dot(weights[1], patches(3, r1, -1, d, STEP), preferred_element_type=F32)
        for j in range(STEP):
            conv[d + j] = y[:, j * LANES : (j + 1) * LANES]
        return 0

    lax.fori_loop(0, ROWS // STEP, backward, 0, unroll=2)

    def finish_backward(q, _):
        rows = pl.ds(pl.multiple_of(q * HALO, HALO), HALO)
        y = jnp.transpose(conv[rows], (1, 0, 2))
        x = feat[:, rows, :].astype(F32)
        s = sigmoid(x)
        slope = maskf[rows, :][None] * (s * (1.0 + x * (1.0 - s)))
        gfeat[:, rows, :] = (cot[:, rows, :].astype(F32) + slope * y).astype(BF16)
        return 0

    lax.fori_loop(0, CHUNKS, finish_backward, 0)
    store_gfeat = pltpu.make_async_copy(gfeat, gfeat_hbm, load.at[1])
    store_gfeat.start()
    for step in range(1, GROUP):
        rank, copy = scatter(step)
        pl.when(rank < PARTS)(copy.wait_send)

    @pl.when(near < PARTS)
    def _():
        for copy in spread:
            copy.wait_send()
        for step in range(1, GROUP):
            gather(step)[1].wait_send()

    for step in range(1, GROUP):
        sender = (near - step + GROUP) % GROUP
        pl.when(sender < PARTS)(gather(step)[1].wait_recv)

    factor = 1.0 / jnp.sqrt(jnp.float32(CELLS))
    last = jnp.concatenate([total[8], total[9]], axis=0) * factor
    for k, ref in enumerate((g1, g2)):
        for p in range(2):
            four = jnp.concatenate([total[4 * k + 2 * p], total[4 * k + 2 * p + 1]], axis=0) * factor
            for t in range(4):
                ref[4 * p + t] = four[:, C * t : C * (t + 1)]
        ref[8] = last[:, C * k : C * (k + 1)]
    gb[...] = jnp.transpose(last[:, 2 * C : 3 * C])[:1]
    store_out.wait()
    store_gfeat.wait()


def hand_over(*refs):
    given, results, held, sems = refs[:5], refs[5:10], refs[10:15], refs[15]
    loads = [pltpu.make_async_copy(given[k], held[k], sems.at[k]) for k in range(5)]
    stores = [pltpu.make_async_copy(held[k], results[k], sems.at[5 + k]) for k in range(5)]
    for copy in loads:
        copy.start()
    for load, store in zip(loads, stores):
        load.wait()
        store.start()
    for copy in stores:
        copy.wait()


def shards(features, cotangent, band_mask, dilation, w_first, b_first, w_second):
    vmem = pl.BlockSpec(memory_space=pltpu.VMEM)
    dma = pltpu.SemaphoreType.DMA
    shape = jax.ShapeDtypeStruct
    field = (C, ROWS, LANES)
    taps = (9, C, C)
    hbm = pl.BlockSpec(memory_space=pltpu.HBM)
    results = pl.pallas_call(
        kernel,
        out_shape=[shape(field, BF16), shape(field, BF16), shape(taps, F32), shape((1, C), F32), shape(taps, F32)],
        in_specs=[pl.BlockSpec(memory_space=pltpu.SMEM)] + [hbm] * 6,
        out_specs=[hbm] * 2 + [vmem] * 3,
        scratch_shapes=[
            pltpu.VMEM(field, BF16),
            pltpu.VMEM(field, BF16),
            pltpu.VMEM(field, BF16),
            pltpu.VMEM(field, BF16),
            pltpu.VMEM((ROWS, LANES), jnp.int32),
            pltpu.VMEM(taps, BF16),
            pltpu.VMEM((1, C), F32),
            pltpu.VMEM(taps, BF16),
            pltpu.VMEM((2, ROWS, C, LANES), BF16),
            pltpu.VMEM((2, ROWS + 2 * PAD, C, LANES), BF16),
            pltpu.VMEM((2, 4, CHUNKS, C, LANES), BF16),
            pltpu.VMEM((4, 3, EXT, C, LANES), BF16),
            pltpu.VMEM((ROWS, LANES), F32),
            pltpu.VMEM((4, C, 9 * C), BF16),
            pltpu.VMEM((C, LANES), F32),
            pltpu.VMEM((ROWS, C, LANES), F32),
            pltpu.VMEM((2, 2, HALO, C, LANES), BF16),
            pltpu.VMEM((2, 4, CHUNKS, C, LANES), BF16),
            pltpu.VMEM((2, 4, C, LANES), BF16),
            pltpu.VMEM((PARTS, HALO, LANES), F32),
            pltpu.VMEM((GROUP, HALO, LANES), F32),
            pltpu.VMEM((GROUP, HALO, LANES), F32),
            pltpu.VMEM((PARTS, HALO, LANES), F32),
            dma((8,)),
            dma((2,)), dma((2,)), dma((2, 4)), dma((2, 4)), dma((2, 4)), dma((2, 4)),
            dma((GROUP,)), dma((GROUP,)), dma((GROUP,)), dma((GROUP,)), dma((GROUP,)), dma((GROUP,)),
        ],
        compiler_params=pltpu.CompilerParams(
            collective_id=0, has_side_effects=True, vmem_limit_bytes=63 * 1024 * 1024
        ),
    )(dilation, features, cotangent, band_mask, jnp.transpose(w_first, (1, 0, 2)), b_first[None],
      jnp.transpose(w_second, (1, 0, 2)))
    out, gfeat, g1, gb, g2 = pl.pallas_call(
        hand_over,
        out_shape=[shape(r.shape, r.dtype) for r in results],
        in_specs=[hbm] * 5,
        out_specs=[hbm] * 5,
        scratch_shapes=[pltpu.VMEM(r.shape, r.dtype) for r in results] + [dma((10,))],
        compiler_params=pltpu.CompilerParams(vmem_limit_bytes=63 * 1024 * 1024),
    )(*results)
    return (out, gfeat, jnp.transpose(g1, (1, 0, 2)), gb[0], jnp.transpose(g2, (1, 0, 2)))


def solution(mesh):
    field, whole = P(None, "diag", "bins"), P()
    return jax.shard_map(
        shards, mesh=mesh, in_specs=(field, field, P("diag", "bins"), whole, whole, whole, whole),
        out_specs=(field, field, whole, whole, whole), check_vma=False)
```

```python
import jax
import jax.numpy as jnp
from jax import lax
from jax.experimental import pallas as pl
from jax.experimental.pallas import tpu as pltpu
from jax.sharding import PartitionSpec as P

F32, BF16 = jnp.float32, jnp.bfloat16
MESH = pl.DeviceIdType.MESH
C = 32
ROWS = 96
LANES = 128
HALO = 16
STRIP = 8
EXT = ROWS + 2 * HALO
CHUNKS = ROWS // HALO
NEAR = 8
GROUP = 16
PART_ROWS = 10
CELLS = 3145728
PAD = 2 * HALO
LAGS = (-2, -1, 0, 1, 2)
ORDER = sorted(range(1, GROUP), key=lambda step: abs(step - GROUP // 2))
TAPS = [(a, b) for a in (-1, 0, 1) for b in (-1, 0, 1)]
SIDE = [(a, b) for a, b in TAPS if a]
CENTER = [(a, b) for a, b in TAPS if not a]
STEP = 4


def sigmoid(v):
    return 0.5 + 0.5 * jnp.tanh(0.5 * v)


def kernel(
    rate, feat_in, cot_in, mask_in, w1_in, b1_in, w2_in,
    out_hbm, gfeat_hbm, g1, gb, g2,
    out, gfeat, feat, cot, mask, w1, b1, w2, center, strips, side, maskf, w_side, w_center, bias, conv, conv_back,
    got_d, got_i, got_c, sums, got, part, total, load,
    send_d, recv_d, send_i, recv_i, send_c, recv_c, send1, recv1, send2, recv2, send3, recv3,
):
    bins, diag = lax.axis_index("bins"), lax.axis_index("diag")
    count = lax.axis_size("bins")
    right, left = (bins + 1) % count, (bins + count - 1) % count
    across = 1 - diag
    near, far = (bins % NEAR) * 2 + diag, bins // NEAR

    def near_peer(step):
        rank = (near + step) % GROUP
        return rank, (far * NEAR + rank // 2, rank % 2)

    def far_peer(step):
        rank = (far + step) % GROUP
        return rank, (rank * NEAR + bins % NEAR, diag)

    peers = [far_peer(s)[1] for s in ORDER] + [near_peer(s)[1] for s in ORDER]
    peers += [(left, diag), (right, diag), (left, across), (right, across)]
    barrier = pltpu.get_barrier_semaphore()
    for peer in peers:
        pl.semaphore_signal(barrier, inc=1, device_id=peer, device_id_type=MESH)

    r1, r2 = rate[0], rate[1]
    lane = lax.broadcasted_iota(jnp.int32, (C, LANES), 1)
    edge_start = (ROWS - HALO) * (1 - diag)
    edge_chunk = (CHUNKS - 1) * (1 - diag)
    halo_start = (ROWS + HALO) * (1 - diag)
    zero_start = (ROWS + HALO) * diag

    edge = pl.ds(pl.multiple_of(edge_start, HALO), HALO)
    rest = pl.ds(pl.multiple_of(HALO * diag, HALO), ROWS - HALO)
    loads = [
        pltpu.make_async_copy(src, dst, load.at[k])
        for k, (src, dst) in enumerate((
            (mask_in, mask),
            (feat_in.at[:, edge], feat.at[:, edge]),
            (cot_in.at[:, edge], cot.at[:, edge]),
            (feat_in.at[:, rest], feat.at[:, rest]),
            (cot_in.at[:, rest], cot.at[:, rest]),
            (w1_in, w1),
            (w2_in, w2),
            (b1_in, b1),
        ))
    ]
    for copy in loads:
        copy.start()
    for field in range(4):
        center[field, :PAD] = jnp.zeros((PAD, C, LANES), BF16)
        center[field, PAD + ROWS :] = jnp.zeros((PAD, C, LANES), BF16)
        for k in range(2):
            side[field, k, pl.ds(zero_start, HALO)] = jnp.zeros((HALO, C, LANES), BF16)
    loads[0].wait()
    maskf[...] = mask[...].astype(F32)

    def enter(q):
        rows = pl.ds(pl.multiple_of(q * HALO, HALO), HALO)
        m = maskf[rows, :][None]
        x = feat[:, rows, :].astype(F32)
        inner = pl.ds(pl.multiple_of(PAD + q * HALO, HALO), HALO)
        center[0, inner] = jnp.transpose((x * sigmoid(x) * m).astype(BF16), (1, 0, 2))
        grad = (cot[:, rows, :].astype(F32) * m).astype(BF16)
        center[1, inner] = jnp.transpose(grad, (1, 0, 2))

    def row_of(field, d):
        return center[field, PAD + d]

    def strip_copy(rnd, side, q):
        return pltpu.make_async_remote_copy(
            src_ref=strips.at[rnd, side, q], dst_ref=got_i.at[rnd, side, q],
            send_sem=send_i.at[rnd, side, q], recv_sem=recv_i.at[rnd, side, q],
            device_id=((right, left)[side], diag), device_id_type=MESH)

    def corner_copy(rnd, side):
        return pltpu.make_async_remote_copy(
            src_ref=strips.at[rnd, side, edge_chunk], dst_ref=got_c.at[rnd, side],
            send_sem=send_c.at[rnd, side], recv_sem=recv_c.at[rnd, side],
            device_id=((right, left)[side], across), device_id_type=MESH)

    def pack(rnd, q):
        for slot in range(2):
            up = jnp.zeros((C, LANES), BF16)
            down = jnp.zeros((C, LANES), BF16)
            for j in range(HALO):
                row = row_of(2 * rnd + slot, q * HALO + j)
                inside = (lane >= STRIP * j) & (lane < STRIP * (j + 1))
                up = jnp.where(inside, pltpu.roll(row, (STRIP * (j + 1)) % LANES, 1), up)
                down = jnp.where(inside, pltpu.roll(row, STRIP * j, 1), down)
            strips[rnd, 0, q, slot] = up
            strips[rnd, 1, q, slot] = down

    def order(n):
        return n + diag * (CHUNKS - 1 - 2 * n)

    def edge_copy(field):
        rnd, slot = field // 2, field % 2
        return pltpu.make_async_remote_copy(
            src_ref=center.at[field, pl.ds(PAD + edge_start, HALO)], dst_ref=got_d.at[rnd, slot],
            send_sem=send_d.at[rnd, slot], recv_sem=recv_d.at[rnd, slot],
            device_id=(bins, across), device_id_type=MESH)

    def settle(rnd, q):
        for side, end in ((0, 0), (1, count - 1)):
            strip_copy(rnd, side, q).wait_recv()

            @pl.when(bins == end)
            def _():
                got_i[rnd, side, q] = jnp.zeros((2, C, LANES), BF16)

    def settle_halo(rnd):
        edge_copy(2 * rnd).wait_recv()
        edge_copy(2 * rnd + 1).wait_recv()
        for side, end in ((0, 0), (1, count - 1)):
            corner_copy(rnd, side).wait_recv()

            @pl.when(bins == end)
            def _():
                got_c[rnd, side] = jnp.zeros((2, C, LANES), BF16)

    def shift_rows(row_of, before, after, r, store):
        for j in range(HALO):
            row = row_of(j)
            low = pltpu.roll(before, (r - STRIP * (j + 1) + LANES) % LANES, 1)
            high = pltpu.roll(after, (2 * LANES - r - STRIP * j) % LANES, 1)
            store(j, 0, jnp.where(lane < r, low, pltpu.roll(row, r, 1)))
            store(j, 1, jnp.where(lane >= LANES - r, high, pltpu.roll(row, LANES - r, 1)))

    def shift(rnd, q, rates):
        for slot in range(2):
            field = 2 * rnd + slot

            def store(j, k, value):
                side[field, k, HALO + q * HALO + j] = value

            shift_rows(lambda j: row_of(field, q * HALO + j), got_i[rnd, 0, q, slot],
                       got_i[rnd, 1, q, slot], rates[slot], store)

    def shift_halo(rnd, rates):
        for slot in range(2):
            field = 2 * rnd + slot

            def store(j, k, value):
                side[field, k, halo_start + j] = value

            rows = got_d.at[rnd, slot]
            center[field, pl.ds(HALO + halo_start, HALO)] = rows[...]
            shift_rows(lambda j: rows[j], got_c[rnd, 0, slot], got_c[rnd, 1, slot], rates[slot], store)

    def patches(taps, field, r, sign, d):
        blocks = []
        for a, b in taps:
            start = HALO + d + sign * (b - a) * r
            if a:
                rows = [side[field, (sign * a + 1) // 2, start + j] for j in range(STEP)]
            else:
                rows = [center[field, HALO + start + j] for j in range(STEP)]
            blocks.append(jnp.concatenate(rows, axis=1))
        return jnp.concatenate(blocks, axis=0)

    def apply(weight, *which):
        taps = [w_center[weight] if w == 0 else w_side[weight] for w in which]
        return taps[0] if len(taps) == 1 else jnp.concatenate(taps, axis=1)

    loads[1].wait()
    loads[2].wait()
    enter(edge_chunk)
    pack(0, edge_chunk)
    loads[3].wait()
    loads[4].wait()

    def enter_more(n, _):
        enter(order(n))
        pack(0, order(n))
        return 0

    ahead = 3
    lax.fori_loop(0, ahead, enter_more, 0)
    pl.semaphore_wait(barrier, len(peers))
    def strips_out(rnd, q):
        for k in range(2):
            strip_copy(rnd, k, q).start()

    def corners_out(rnd):
        for k in range(2):
            corner_copy(rnd, k).start()

    def first_strips(n, _):
        strips_out(0, order(n))
        return 0

    corners_out(0)
    lax.fori_loop(0, ahead, first_strips, 0)
    strips_out(0, edge_chunk)
    edge_copy(0).start()

    def enter_rest(n, _):
        enter_more(n, 0)
        strips_out(0, order(n))
        return 0

    lax.fori_loop(ahead, CHUNKS - 1, enter_rest, 0)
    edge_copy(1).start()

    for copy in loads[5:]:
        copy.wait()
    bias[...] = jnp.broadcast_to(jnp.transpose(jnp.broadcast_to(b1[...], (C, C)))[:, :1], (C, LANES))
    for k, ref in enumerate((w1, w2)):
        taps = [ref[t] for t in range(9)]
        turned = [jnp.transpose(t.astype(F32)).astype(BF16) for t in taps]
        for m, blocks in ((2 * k, taps), (2 * k + 1, turned)):
            w_side[m] = jnp.concatenate(blocks[:3] + blocks[6:], axis=1)
            w_center[m] = jnp.concatenate(blocks[3:6], axis=1)

    def middle_center(q):
        for step in range(HALO // STEP):
            d = q * HALO + step * STEP
            pre = jnp.dot(w_center[0], patches(CENTER, 0, r1, 1, d), preferred_element_type=F32)
            back = jnp.dot(w_center[3], patches(CENTER, 1, r2, -1, d), preferred_element_type=F32)
            for j in range(STEP):
                conv[d + j] = pre[:, j * LANES : (j + 1) * LANES] + bias[...]
                conv_back[d + j] = back[:, j * LANES : (j + 1) * LANES]

    def middle(d):
        pre = jnp.dot(w_side[0], patches(SIDE, 0, r1, 1, d), preferred_element_type=F32)
        back = jnp.dot(w_side[3], patches(SIDE, 1, r2, -1, d), preferred_element_type=F32)
        for j in range(STEP):
            m = maskf[pl.ds(d + j, 1), :]
            y = pre[:, j * LANES : (j + 1) * LANES] + conv[d + j]
            s = sigmoid(y)
            center[2, PAD + d + j] = (y * s * m).astype(BF16)
            grad = back[:, j * LANES : (j + 1) * LANES] + conv_back[d + j]
            center[3, PAD + d + j] = (grad * m * (s * (1.0 + y * (1.0 - s)))).astype(BF16)

    def center_step(n, _):
        middle_center(order(n))
        return 0

    lax.fori_loop(0, CHUNKS - 1, center_step, 0)

    def middle_chunk(q):
        for step in range(HALO // STEP):
            middle(q * HALO + step * STEP)

    settle(0, order(0))
    shift(0, order(0), (r1, r2))

    def middle_step(n, _):
        settle(0, order(n + 1))
        shift(0, order(n + 1), (r1, r2))
        middle_chunk(order(n))
        return 0

    lax.fori_loop(0, CHUNKS - 1, middle_step, 0)
    settle_halo(0)
    shift_halo(0, (r1, r2))
    middle_center(edge_chunk)
    middle_chunk(edge_chunk)
    edge_copy(2).start()

    wide = 32
    nt = (((1,), (1,)), ((), ()))

    def row_block(rows):
        return jnp.concatenate(rows, axis=1)

    def near_rows(field, k):
        before = row_block([side[field, 0, k + j] for j in range(wide)])
        same = row_block([center[field, HALO + k + j] for j in range(wide)])
        return [before, same, row_block([side[field, 1, k + j] for j in range(wide)])]

    def grads(n, carry):
        k = n * wide
        act = near_rows(0, k)
        act.append(jnp.ones((C, wide * LANES), BF16))
        ups = [row_block([center[3, HALO + k - m * r1 + j] for j in range(wide)]) for m in LAGS]
        one = lax.dot_general(jnp.concatenate(ups, axis=0), jnp.concatenate(act, axis=0), nt,
                              preferred_element_type=F32)
        grad = near_rows(1, k)
        hid = [row_block([center[2, HALO + k + m * r2 + j] for j in range(wide)]) for m in LAGS]
        two = lax.dot_general(jnp.concatenate(grad, axis=0), jnp.concatenate(hid, axis=0), nt,
                              preferred_element_type=F32)
        return carry[0] + one, carry[1] + two

    zero = (jnp.zeros((5 * C, 4 * C), F32), jnp.zeros((3 * C, 5 * C), F32))
    one, two = lax.fori_loop(0, EXT // wide, grads, zero, unroll=2)

    def block(value, i, j):
        return value[C * i : C * (i + 1), C * j : C * (j + 1)]

    blocks = [[block(one, b - a + 2, a + 1) for a, b in TAPS], [block(two, 1 - a, b - a + 2) for a, b in TAPS]]
    rows = [jnp.concatenate(blocks[k][4 * p : 4 * p + 4], axis=1) for k in range(2) for p in range(2)]
    rows.append(jnp.concatenate([blocks[0][8], blocks[1][8], block(one, 2, 3), jnp.zeros((C, C), F32)], axis=1))
    rows = jnp.concatenate(rows, axis=0)
    for k in range(GROUP):
        sums[k] = rows[PART_ROWS * k : PART_ROWS * (k + 1)]

    def scatter(step):
        rank, device = near_peer(step)
        return rank, pltpu.make_async_remote_copy(
            src_ref=sums.at[rank], dst_ref=got.at[step], send_sem=send1.at[step],
            recv_sem=recv1.at[step], device_id=device, device_id_type=MESH)

    for step in ORDER:
        scatter(step)[1].start()
    edge_copy(3).start()

    pack(1, edge_chunk)
    strips_out(1, edge_chunk)
    corners_out(1)

    def launch_rest(n, _):
        pack(1, order(n))
        strips_out(1, order(n))
        return 0

    lax.fori_loop(0, CHUNKS - 1, launch_rest, 0)

    spread = []
    for step in ORDER:
        rank, device = far_peer(step)
        spread.append(pltpu.make_async_remote_copy(
            src_ref=part.at[far], dst_ref=part.at[far], send_sem=send2.at[step],
            recv_sem=recv2.at[step], device_id=device, device_id_type=MESH))

    value = sums[near]
    for step in ORDER:
        scatter(step)[1].wait_recv()
        value = value + got[step]
    part[far] = value
    for copy in spread:
        copy.start()

    def last_conv(weight, field, r, sign, q):
        for step in range(HALO // STEP):
            d = q * HALO + step * STEP
            taps = patches(SIDE + CENTER, field, r, sign, d)
            y = jnp.dot(apply(weight, 1, 0), taps, preferred_element_type=F32)
            for j in range(STEP):
                conv[d + j] = y[:, j * LANES : (j + 1) * LANES]

    settle(1, order(0))
    shift(1, order(0), (r2, r1))

    def forward(n, _):
        settle(1, order(n + 1))
        shift(1, order(n + 1), (r2, r1))
        last_conv(2, 2, r2, 1, order(n))
        return 0

    lax.fori_loop(0, CHUNKS - 1, forward, 0)
    settle_halo(1)
    shift_halo(1, (r2, r1))
    last_conv(2, 2, r2, 1, edge_chunk)

    def finish_forward(q, _):
        rows = pl.ds(pl.multiple_of(q * HALO, HALO), HALO)
        y = jnp.transpose(conv[rows], (1, 0, 2))
        out[:, rows, :] = (feat[:, rows, :].astype(F32) + maskf[rows, :][None] * y).astype(BF16)
        return 0

    lax.fori_loop(0, CHUNKS, finish_forward, 0)
    store_out = pltpu.make_async_copy(out, out_hbm, load.at[0])
    store_out.start()
    def gather(step):
        return near_peer(step)[0], pltpu.make_async_remote_copy(
            src_ref=total.at[near], dst_ref=total.at[near], send_sem=send3.at[step],
            recv_sem=recv3.at[step], device_id=near_peer(step)[1], device_id_type=MESH)

    for copy in spread:
        copy.wait_recv()
    value = part[0]
    for rank in range(1, GROUP):
        value = value + part[rank]
    total[near] = value
    for step in ORDER:
        gather(step)[1].start()

    def backward(q, _):
        last_conv(1, 3, r1, -1, q)
        return 0

    lax.fori_loop(0, CHUNKS, backward, 0)

    def finish_backward(q, _):
        rows = pl.ds(pl.multiple_of(q * HALO, HALO), HALO)
        y = jnp.transpose(conv[rows], (1, 0, 2))
        x = feat[:, rows, :].astype(F32)
        s = sigmoid(x)
        slope = maskf[rows, :][None] * (s * (1.0 + x * (1.0 - s)))
        gfeat[:, rows, :] = (cot[:, rows, :].astype(F32) + slope * y).astype(BF16)
        return 0

    lax.fori_loop(0, CHUNKS, finish_backward, 0)
    store_gfeat = pltpu.make_async_copy(gfeat, gfeat_hbm, load.at[1])
    store_gfeat.start()
    for field in range(4):
        edge_copy(field).wait_send()

    def sent(q, _):
        for rnd in range(2):
            for side in range(2):
                strip_copy(rnd, side, q).wait_send()
        return 0

    lax.fori_loop(0, CHUNKS, sent, 0)
    for rnd in range(2):
        for side in range(2):
            corner_copy(rnd, side).wait_send()
    for step in ORDER:
        scatter(step)[1].wait_send()
    for copy in spread:
        copy.wait_send()
    for step in ORDER:
        gather(step)[1].wait()

    factor = 1.0 / jnp.sqrt(jnp.float32(CELLS))
    rows = jnp.concatenate([total[k] for k in range(GROUP)], axis=0) * factor
    last = rows[4 * C :]
    for k, ref in enumerate((g1, g2)):
        for t in range(8):
            base = C * (2 * k + t // 4)
            ref[t] = rows[base : base + C, C * (t % 4) : C * (t % 4 + 1)]
        ref[8] = last[:, C * k : C * (k + 1)]
    gb[...] = jnp.transpose(last[:, 2 * C : 3 * C])[:1]
    store_out.wait()
    store_gfeat.wait()


def hand_over(*refs):
    given, results, held, sems = refs[:5], refs[5:10], refs[10:15], refs[15]
    loads = [pltpu.make_async_copy(given[k], held[k], sems.at[k]) for k in range(5)]
    stores = [pltpu.make_async_copy(held[k], results[k], sems.at[5 + k]) for k in range(5)]
    for copy in loads:
        copy.start()
    for load, store in zip(loads, stores):
        load.wait()
        store.start()
    for copy in stores:
        copy.wait()


def shards(features, cotangent, band_mask, dilation, w_first, b_first, w_second):
    vmem = pl.BlockSpec(memory_space=pltpu.VMEM)
    dma = pltpu.SemaphoreType.DMA
    shape = jax.ShapeDtypeStruct
    field = (C, ROWS, LANES)
    taps = (9, C, C)
    hbm = pl.BlockSpec(memory_space=pltpu.HBM)
    results = pl.pallas_call(
        kernel,
        out_shape=[shape(field, BF16), shape(field, BF16), shape(taps, F32), shape((1, C), F32), shape(taps, F32)],
        in_specs=[pl.BlockSpec(memory_space=pltpu.SMEM)] + [hbm] * 6,
        out_specs=[hbm] * 2 + [vmem] * 3,
        scratch_shapes=[
            pltpu.VMEM(field, BF16),
            pltpu.VMEM(field, BF16),
            pltpu.VMEM(field, BF16),
            pltpu.VMEM(field, BF16),
            pltpu.VMEM((ROWS, LANES), jnp.int32),
            pltpu.VMEM(taps, BF16),
            pltpu.VMEM((1, C), F32),
            pltpu.VMEM(taps, BF16),
            pltpu.VMEM((4, ROWS + 2 * PAD, C, LANES), BF16),
            pltpu.VMEM((2, 2, CHUNKS, 2, C, LANES), BF16),
            pltpu.VMEM((4, 2, EXT, C, LANES), BF16),
            pltpu.VMEM((ROWS, LANES), F32),
            pltpu.VMEM((4, C, 6 * C), BF16),
            pltpu.VMEM((4, C, 3 * C), BF16),
            pltpu.VMEM((C, LANES), F32),
            pltpu.VMEM((ROWS, C, LANES), F32),
            pltpu.VMEM((ROWS, C, LANES), F32),
            pltpu.VMEM((2, 2, HALO, C, LANES), BF16),
            pltpu.VMEM((2, 2, CHUNKS, 2, C, LANES), BF16),
            pltpu.VMEM((2, 2, 2, C, LANES), BF16),
            pltpu.VMEM((GROUP, PART_ROWS, LANES), F32),
            pltpu.VMEM((GROUP, PART_ROWS, LANES), F32),
            pltpu.VMEM((GROUP, PART_ROWS, LANES), F32),
            pltpu.VMEM((GROUP, PART_ROWS, LANES), F32),
            dma((8,)),
            dma((2, 2)), dma((2, 2)), dma((2, 2, CHUNKS)), dma((2, 2, CHUNKS)), dma((2, 2)), dma((2, 2)),
            dma((GROUP,)), dma((GROUP,)), dma((GROUP,)), dma((GROUP,)), dma((GROUP,)), dma((GROUP,)),
        ],
        compiler_params=pltpu.CompilerParams(
            collective_id=0, has_side_effects=True, vmem_limit_bytes=63 * 1024 * 1024
        ),
    )(dilation, features, cotangent, band_mask, jnp.transpose(w_first, (1, 0, 2)), b_first[None],
      jnp.transpose(w_second, (1, 0, 2)))
    out, gfeat, g1, gb, g2 = pl.pallas_call(
        hand_over,
        out_shape=[shape(r.shape, r.dtype) for r in results],
        in_specs=[hbm] * 5,
        out_specs=[hbm] * 5,
        scratch_shapes=[pltpu.VMEM(r.shape, r.dtype) for r in results] + [dma((10,))],
        compiler_params=pltpu.CompilerParams(vmem_limit_bytes=63 * 1024 * 1024),
    )(*results)
    return (out, gfeat, jnp.transpose(g1, (1, 0, 2)), gb[0], jnp.transpose(g2, (1, 0, 2)))


def solution(mesh):
    field, whole = P(None, "diag", "bins"), P()
    return jax.shard_map(
        shards, mesh=mesh, in_specs=(field, field, P("diag", "bins"), whole, whole, whole, whole),
        out_specs=(field, field, whole, whole, whole), check_vma=False)
```

```python
import jax
import jax.numpy as jnp
from jax import lax
from jax.experimental import pallas as pl
from jax.experimental.pallas import tpu as pltpu
from jax.sharding import PartitionSpec as P

F32, BF16 = jnp.float32, jnp.bfloat16
MESH = pl.DeviceIdType.MESH
C = 32
ROWS = 96
LANES = 128
HALO = 16
STRIP = 8
EXT = ROWS + 2 * HALO
CHUNKS = ROWS // HALO
NEAR = 8
GROUP = 16
PART_ROWS = 10
CELLS = 3145728
PAD = 2 * HALO
LAGS = (-2, -1, 0, 1, 2)
ORDER = sorted(range(1, GROUP), key=lambda step: abs(step - GROUP // 2))
TAPS = [(a, b) for a in (-1, 0, 1) for b in (-1, 0, 1)]
SIDE = [(a, b) for a, b in TAPS if a]
CENTER = [(a, b) for a, b in TAPS if not a]
STEP = 4


def sigmoid(v):
    return 0.5 + 0.5 * jnp.tanh(0.5 * v)


def kernel(
    rate, feat_in, cot_in, mask_in, w1_in, b1_in, w2_in,
    out, gfeat, g1, gb, g2,
    feat, cot, mask, w1, b1, w2, center, strips, side, maskf, w_side, w_center, bias, conv, conv_back,
    got_d, got_i, got_c, sums, got, part, total, load,
    send_d, recv_d, send_i, recv_i, send_c, recv_c, send1, recv1, send2, recv2, send3, recv3,
):
    bins, diag = lax.axis_index("bins"), lax.axis_index("diag")
    count = lax.axis_size("bins")
    right, left = (bins + 1) % count, (bins + count - 1) % count
    across = 1 - diag
    near, far = (bins % NEAR) * 2 + diag, bins // NEAR

    def near_peer(step):
        rank = (near + step) % GROUP
        return rank, (far * NEAR + rank // 2, rank % 2)

    def far_peer(step):
        rank = (far + step) % GROUP
        return rank, (rank * NEAR + bins % NEAR, diag)

    peers = [far_peer(s)[1] for s in ORDER] + [near_peer(s)[1] for s in ORDER]
    peers += [(left, diag), (right, diag), (left, across), (right, across)]
    barrier = pltpu.get_barrier_semaphore()
    for peer in peers:
        pl.semaphore_signal(barrier, inc=1, device_id=peer, device_id_type=MESH)

    r1, r2 = rate[0], rate[1]
    lane = lax.broadcasted_iota(jnp.int32, (C, LANES), 1)
    edge_start = (ROWS - HALO) * (1 - diag)
    edge_chunk = (CHUNKS - 1) * (1 - diag)
    halo_start = (ROWS + HALO) * (1 - diag)
    zero_start = (ROWS + HALO) * diag

    edge = pl.ds(pl.multiple_of(edge_start, HALO), HALO)
    rest = pl.ds(pl.multiple_of(HALO * diag, HALO), ROWS - HALO)
    loads = [
        pltpu.make_async_copy(src, dst, load.at[k])
        for k, (src, dst) in enumerate((
            (mask_in, mask),
            (feat_in.at[:, edge], feat.at[:, edge]),
            (cot_in.at[:, edge], cot.at[:, edge]),
            (feat_in.at[:, rest], feat.at[:, rest]),
            (cot_in.at[:, rest], cot.at[:, rest]),
            (w1_in, w1),
            (w2_in, w2),
            (b1_in, b1),
        ))
    ]
    for copy in loads:
        copy.start()
    for field in range(4):
        center[field, :PAD] = jnp.zeros((PAD, C, LANES), BF16)
        center[field, PAD + ROWS :] = jnp.zeros((PAD, C, LANES), BF16)
        for k in range(2):
            side[field, k, pl.ds(zero_start, HALO)] = jnp.zeros((HALO, C, LANES), BF16)
    loads[0].wait()
    maskf[...] = mask[...].astype(F32)

    def enter(q):
        rows = pl.ds(pl.multiple_of(q * HALO, HALO), HALO)
        m = maskf[rows, :][None]
        x = feat[:, rows, :].astype(F32)
        inner = pl.ds(pl.multiple_of(PAD + q * HALO, HALO), HALO)
        center[0, inner] = jnp.transpose((x * sigmoid(x) * m).astype(BF16), (1, 0, 2))
        grad = (cot[:, rows, :].astype(F32) * m).astype(BF16)
        center[1, inner] = jnp.transpose(grad, (1, 0, 2))

    def row_of(field, d):
        return center[field, PAD + d]

    def strip_copy(rnd, side, q):
        return pltpu.make_async_remote_copy(
            src_ref=strips.at[rnd, side, q], dst_ref=got_i.at[rnd, side, q],
            send_sem=send_i.at[rnd, side, q], recv_sem=recv_i.at[rnd, side, q],
            device_id=((right, left)[side], diag), device_id_type=MESH)

    def corner_copy(rnd, side):
        return pltpu.make_async_remote_copy(
            src_ref=strips.at[rnd, side, edge_chunk], dst_ref=got_c.at[rnd, side],
            send_sem=send_c.at[rnd, side], recv_sem=recv_c.at[rnd, side],
            device_id=((right, left)[side], across), device_id_type=MESH)

    def pack(rnd, q):
        for slot in range(2):
            up = jnp.zeros((C, LANES), BF16)
            down = jnp.zeros((C, LANES), BF16)
            for j in range(HALO):
                row = row_of(2 * rnd + slot, q * HALO + j)
                inside = (lane >= STRIP * j) & (lane < STRIP * (j + 1))
                up = jnp.where(inside, pltpu.roll(row, (STRIP * (j + 1)) % LANES, 1), up)
                down = jnp.where(inside, pltpu.roll(row, STRIP * j, 1), down)
            strips[rnd, 0, q, slot] = up
            strips[rnd, 1, q, slot] = down

    def order(n):
        return n + diag * (CHUNKS - 1 - 2 * n)

    def edge_copy(field):
        rnd, slot = field // 2, field % 2
        return pltpu.make_async_remote_copy(
            src_ref=center.at[field, pl.ds(PAD + edge_start, HALO)], dst_ref=got_d.at[rnd, slot],
            send_sem=send_d.at[rnd, slot], recv_sem=recv_d.at[rnd, slot],
            device_id=(bins, across), device_id_type=MESH)

    def settle(rnd, q):
        for side, end in ((0, 0), (1, count - 1)):
            strip_copy(rnd, side, q).wait_recv()

            @pl.when(bins == end)
            def _():
                got_i[rnd, side, q] = jnp.zeros((2, C, LANES), BF16)

    def settle_halo(rnd):
        edge_copy(2 * rnd).wait_recv()
        edge_copy(2 * rnd + 1).wait_recv()
        for side, end in ((0, 0), (1, count - 1)):
            corner_copy(rnd, side).wait_recv()

            @pl.when(bins == end)
            def _():
                got_c[rnd, side] = jnp.zeros((2, C, LANES), BF16)

    def shift_rows(row_of, before, after, r, store):
        for j in range(HALO):
            row = row_of(j)
            low = pltpu.roll(before, (r - STRIP * (j + 1) + LANES) % LANES, 1)
            high = pltpu.roll(after, (2 * LANES - r - STRIP * j) % LANES, 1)
            store(j, 0, jnp.where(lane < r, low, pltpu.roll(row, r, 1)))
            store(j, 1, jnp.where(lane >= LANES - r, high, pltpu.roll(row, LANES - r, 1)))

    def shift(rnd, q, rates):
        for slot in range(2):
            field = 2 * rnd + slot

            def store(j, k, value):
                side[field, k, HALO + q * HALO + j] = value

            shift_rows(lambda j: row_of(field, q * HALO + j), got_i[rnd, 0, q, slot],
                       got_i[rnd, 1, q, slot], rates[slot], store)

    def shift_halo(rnd, rates):
        for slot in range(2):
            field = 2 * rnd + slot

            def store(j, k, value):
                side[field, k, halo_start + j] = value

            rows = got_d.at[rnd, slot]
            center[field, pl.ds(HALO + halo_start, HALO)] = rows[...]
            shift_rows(lambda j: rows[j], got_c[rnd, 0, slot], got_c[rnd, 1, slot], rates[slot], store)

    def patches(taps, field, r, sign, d):
        blocks = []
        for a, b in taps:
            start = HALO + d + sign * (b - a) * r
            if a:
                rows = [side[field, (sign * a + 1) // 2, start + j] for j in range(STEP)]
            else:
                rows = [center[field, HALO + start + j] for j in range(STEP)]
            blocks.append(jnp.concatenate(rows, axis=1))
        return jnp.concatenate(blocks, axis=0)

    def apply(weight, *which):
        taps = [w_center[weight] if w == 0 else w_side[weight] for w in which]
        return taps[0] if len(taps) == 1 else jnp.concatenate(taps, axis=1)

    loads[1].wait()
    loads[2].wait()
    enter(edge_chunk)
    pack(0, edge_chunk)
    loads[3].wait()
    loads[4].wait()

    def enter_more(n, _):
        enter(order(n))
        pack(0, order(n))
        return 0

    ahead = 3
    lax.fori_loop(0, ahead, enter_more, 0)
    pl.semaphore_wait(barrier, len(peers))
    def strips_out(rnd, q):
        for k in range(2):
            strip_copy(rnd, k, q).start()

    def corners_out(rnd):
        for k in range(2):
            corner_copy(rnd, k).start()

    def first_strips(n, _):
        strips_out(0, order(n))
        return 0

    corners_out(0)
    lax.fori_loop(0, ahead, first_strips, 0)
    strips_out(0, edge_chunk)
    edge_copy(0).start()

    def enter_rest(n, _):
        enter_more(n, 0)
        strips_out(0, order(n))
        return 0

    lax.fori_loop(ahead, CHUNKS - 1, enter_rest, 0)
    edge_copy(1).start()

    for copy in loads[5:]:
        copy.wait()
    bias[...] = jnp.broadcast_to(jnp.transpose(jnp.broadcast_to(b1[...], (C, C)))[:, :1], (C, LANES))
    for k, ref in enumerate((w1, w2)):
        taps = [ref[t] for t in range(9)]
        turned = [jnp.transpose(t.astype(F32)).astype(BF16) for t in taps]
        for m, blocks in ((2 * k, taps), (2 * k + 1, turned)):
            w_side[m] = jnp.concatenate(blocks[:3] + blocks[6:], axis=1)
            w_center[m] = jnp.concatenate(blocks[3:6], axis=1)

    def middle_center(q):
        for step in range(HALO // STEP):
            d = q * HALO + step * STEP
            pre = jnp.dot(w_center[0], patches(CENTER, 0, r1, 1, d), preferred_element_type=F32)
            back = jnp.dot(w_center[3], patches(CENTER, 1, r2, -1, d), preferred_element_type=F32)
            for j in range(STEP):
                conv[d + j] = pre[:, j * LANES : (j + 1) * LANES] + bias[...]
                conv_back[d + j] = back[:, j * LANES : (j + 1) * LANES]

    def middle(d):
        pre = jnp.dot(w_side[0], patches(SIDE, 0, r1, 1, d), preferred_element_type=F32)
        back = jnp.dot(w_side[3], patches(SIDE, 1, r2, -1, d), preferred_element_type=F32)
        for j in range(STEP):
            m = maskf[pl.ds(d + j, 1), :]
            y = pre[:, j * LANES : (j + 1) * LANES] + conv[d + j]
            s = sigmoid(y)
            center[2, PAD + d + j] = (y * s * m).astype(BF16)
            grad = back[:, j * LANES : (j + 1) * LANES] + conv_back[d + j]
            center[3, PAD + d + j] = (grad * m * (s * (1.0 + y * (1.0 - s)))).astype(BF16)

    def center_step(n, _):
        middle_center(order(n))
        return 0

    lax.fori_loop(0, CHUNKS - 1, center_step, 0)

    def middle_chunk(q):
        for step in range(HALO // STEP):
            middle(q * HALO + step * STEP)

    settle(0, order(0))
    shift(0, order(0), (r1, r2))

    def middle_step(n, _):
        settle(0, order(n + 1))
        shift(0, order(n + 1), (r1, r2))
        middle_chunk(order(n))
        return 0

    lax.fori_loop(0, CHUNKS - 1, middle_step, 0)
    settle_halo(0)
    shift_halo(0, (r1, r2))
    middle_center(edge_chunk)
    middle_chunk(edge_chunk)
    edge_copy(2).start()

    wide = 32
    nt = (((1,), (1,)), ((), ()))

    def row_block(rows):
        return jnp.concatenate(rows, axis=1)

    def near_rows(field, k):
        before = row_block([side[field, 0, k + j] for j in range(wide)])
        same = row_block([center[field, HALO + k + j] for j in range(wide)])
        return [before, same, row_block([side[field, 1, k + j] for j in range(wide)])]

    def grads(n, carry):
        k = n * wide
        act = near_rows(0, k)
        act.append(jnp.ones((C, wide * LANES), BF16))
        ups = [row_block([center[3, HALO + k - m * r1 + j] for j in range(wide)]) for m in LAGS]
        one = lax.dot_general(jnp.concatenate(ups, axis=0), jnp.concatenate(act, axis=0), nt,
                              preferred_element_type=F32)
        grad = near_rows(1, k)
        hid = [row_block([center[2, HALO + k + m * r2 + j] for j in range(wide)]) for m in LAGS]
        two = lax.dot_general(jnp.concatenate(grad, axis=0), jnp.concatenate(hid, axis=0), nt,
                              preferred_element_type=F32)
        return carry[0] + one, carry[1] + two

    zero = (jnp.zeros((5 * C, 4 * C), F32), jnp.zeros((3 * C, 5 * C), F32))
    one, two = lax.fori_loop(0, EXT // wide, grads, zero, unroll=2)

    def block(value, i, j):
        return value[C * i : C * (i + 1), C * j : C * (j + 1)]

    blocks = [[block(one, b - a + 2, a + 1) for a, b in TAPS], [block(two, 1 - a, b - a + 2) for a, b in TAPS]]
    rows = [jnp.concatenate(blocks[k][4 * p : 4 * p + 4], axis=1) for k in range(2) for p in range(2)]
    rows.append(jnp.concatenate([blocks[0][8], blocks[1][8], block(one, 2, 3), jnp.zeros((C, C), F32)], axis=1))
    rows = jnp.concatenate(rows, axis=0)
    for k in range(GROUP):
        sums[k] = rows[PART_ROWS * k : PART_ROWS * (k + 1)]

    def scatter(step):
        rank, device = near_peer(step)
        return rank, pltpu.make_async_remote_copy(
            src_ref=sums.at[rank], dst_ref=got.at[step], send_sem=send1.at[step],
            recv_sem=recv1.at[step], device_id=device, device_id_type=MESH)

    for step in ORDER:
        scatter(step)[1].start()
    edge_copy(3).start()

    pack(1, edge_chunk)
    strips_out(1, edge_chunk)
    corners_out(1)

    def launch_rest(n, _):
        pack(1, order(n))
        strips_out(1, order(n))
        return 0

    lax.fori_loop(0, CHUNKS - 1, launch_rest, 0)

    spread = []
    for step in ORDER:
        rank, device = far_peer(step)
        spread.append(pltpu.make_async_remote_copy(
            src_ref=part.at[far], dst_ref=part.at[far], send_sem=send2.at[step],
            recv_sem=recv2.at[step], device_id=device, device_id_type=MESH))

    value = sums[near]
    for step in ORDER:
        scatter(step)[1].wait_recv()
        value = value + got[step]
    part[far] = value
    for copy in spread:
        copy.start()

    def last_conv(weight, field, r, sign, q):
        for step in range(HALO // STEP):
            d = q * HALO + step * STEP
            taps = patches(SIDE + CENTER, field, r, sign, d)
            y = jnp.dot(apply(weight, 1, 0), taps, preferred_element_type=F32)
            for j in range(STEP):
                conv[d + j] = y[:, j * LANES : (j + 1) * LANES]

    settle(1, order(0))
    shift(1, order(0), (r2, r1))

    def forward(n, _):
        settle(1, order(n + 1))
        shift(1, order(n + 1), (r2, r1))
        last_conv(2, 2, r2, 1, order(n))
        return 0

    lax.fori_loop(0, CHUNKS - 1, forward, 0)
    settle_halo(1)
    shift_halo(1, (r2, r1))
    last_conv(2, 2, r2, 1, edge_chunk)

    def finish_forward(q, _):
        rows = pl.ds(pl.multiple_of(q * HALO, HALO), HALO)
        y = jnp.transpose(conv[rows], (1, 0, 2))
        out[:, rows, :] = (feat[:, rows, :].astype(F32) + maskf[rows, :][None] * y).astype(BF16)
        return 0

    lax.fori_loop(0, CHUNKS, finish_forward, 0)
    def gather(step):
        return near_peer(step)[0], pltpu.make_async_remote_copy(
            src_ref=total.at[near], dst_ref=total.at[near], send_sem=send3.at[step],
            recv_sem=recv3.at[step], device_id=near_peer(step)[1], device_id_type=MESH)

    for copy in spread:
        copy.wait_recv()
    value = part[0]
    for rank in range(1, GROUP):
        value = value + part[rank]
    total[near] = value
    for step in ORDER:
        gather(step)[1].start()

    def backward(q, _):
        last_conv(1, 3, r1, -1, q)
        return 0

    lax.fori_loop(0, CHUNKS, backward, 0)

    def finish_backward(q, _):
        rows = pl.ds(pl.multiple_of(q * HALO, HALO), HALO)
        y = jnp.transpose(conv[rows], (1, 0, 2))
        x = feat[:, rows, :].astype(F32)
        s = sigmoid(x)
        slope = maskf[rows, :][None] * (s * (1.0 + x * (1.0 - s)))
        gfeat[:, rows, :] = (cot[:, rows, :].astype(F32) + slope * y).astype(BF16)
        return 0

    lax.fori_loop(0, CHUNKS, finish_backward, 0)
    for field in range(4):
        edge_copy(field).wait_send()

    def sent(q, _):
        for rnd in range(2):
            for side in range(2):
                strip_copy(rnd, side, q).wait_send()
        return 0

    lax.fori_loop(0, CHUNKS, sent, 0)
    for rnd in range(2):
        for side in range(2):
            corner_copy(rnd, side).wait_send()
    for step in ORDER:
        scatter(step)[1].wait_send()
    for copy in spread:
        copy.wait_send()
    for step in ORDER:
        gather(step)[1].wait()

    factor = 1.0 / jnp.sqrt(jnp.float32(CELLS))
    rows = jnp.concatenate([total[k] for k in range(GROUP)], axis=0) * factor
    last = rows[4 * C :]
    for k, ref in enumerate((g1, g2)):
        for t in range(8):
            base = C * (2 * k + t // 4)
            ref[t] = rows[base : base + C, C * (t % 4) : C * (t % 4 + 1)]
        ref[8] = last[:, C * k : C * (k + 1)]
    gb[...] = jnp.transpose(last[:, 2 * C : 3 * C])[:1]


def hand_over(*refs):
    given, results, sems = refs[:5], refs[5:10], refs[10]
    copies = [pltpu.make_async_copy(given[k], results[k], sems.at[k]) for k in range(5)]
    for copy in copies:
        copy.start()
    for copy in copies:
        copy.wait()


def shards(features, cotangent, band_mask, dilation, w_first, b_first, w_second):
    vmem = pl.BlockSpec(memory_space=pltpu.VMEM)
    dma = pltpu.SemaphoreType.DMA
    shape = jax.ShapeDtypeStruct
    field = (C, ROWS, LANES)
    taps = (9, C, C)
    hbm = pl.BlockSpec(memory_space=pltpu.HBM)
    results = pl.pallas_call(
        kernel,
        out_shape=[pltpu.VMEM(field, BF16), pltpu.VMEM(field, BF16), pltpu.VMEM(taps, F32), pltpu.VMEM((1, C), F32), pltpu.VMEM(taps, F32)],
        in_specs=[pl.BlockSpec(memory_space=pltpu.SMEM)] + [hbm] * 6,
        out_specs=[vmem] * 5,
        scratch_shapes=[
            pltpu.VMEM(field, BF16),
            pltpu.VMEM(field, BF16),
            pltpu.VMEM((ROWS, LANES), jnp.int32),
            pltpu.VMEM(taps, BF16),
            pltpu.VMEM((1, C), F32),
            pltpu.VMEM(taps, BF16),
            pltpu.VMEM((4, ROWS + 2 * PAD, C, LANES), BF16),
            pltpu.VMEM((2, 2, CHUNKS, 2, C, LANES), BF16),
            pltpu.VMEM((4, 2, EXT, C, LANES), BF16),
            pltpu.VMEM((ROWS, LANES), F32),
            pltpu.VMEM((4, C, 6 * C), BF16),
            pltpu.VMEM((4, C, 3 * C), BF16),
            pltpu.VMEM((C, LANES), F32),
            pltpu.VMEM((ROWS, C, LANES), F32),
            pltpu.VMEM((ROWS, C, LANES), F32),
            pltpu.VMEM((2, 2, HALO, C, LANES), BF16),
            pltpu.VMEM((2, 2, CHUNKS, 2, C, LANES), BF16),
            pltpu.VMEM((2, 2, 2, C, LANES), BF16),
            pltpu.VMEM((GROUP, PART_ROWS, LANES), F32),
            pltpu.VMEM((GROUP, PART_ROWS, LANES), F32),
            pltpu.VMEM((GROUP, PART_ROWS, LANES), F32),
            pltpu.VMEM((GROUP, PART_ROWS, LANES), F32),
            dma((8,)),
            dma((2, 2)), dma((2, 2)), dma((2, 2, CHUNKS)), dma((2, 2, CHUNKS)), dma((2, 2)), dma((2, 2)),
            dma((GROUP,)), dma((GROUP,)), dma((GROUP,)), dma((GROUP,)), dma((GROUP,)), dma((GROUP,)),
        ],
        compiler_params=pltpu.CompilerParams(
            collective_id=0, has_side_effects=True, vmem_limit_bytes=61 * 1024 * 1024
        ),
    )(dilation, features, cotangent, band_mask, jnp.transpose(w_first, (1, 0, 2)), b_first[None],
      jnp.transpose(w_second, (1, 0, 2)))
    out, gfeat, g1, gb, g2 = pl.pallas_call(
        hand_over,
        out_shape=[shape(r.shape, r.dtype) for r in results],
        in_specs=[vmem] * 5,
        out_specs=[hbm] * 5,
        scratch_shapes=[dma((5,))],
        compiler_params=pltpu.CompilerParams(vmem_limit_bytes=8 * 1024 * 1024),
    )(*results)
    return (out, gfeat, jnp.transpose(g1, (1, 0, 2)), gb[0], jnp.transpose(g2, (1, 0, 2)))


def solution(mesh):
    field, whole = P(None, "diag", "bins"), P()
    return jax.shard_map(
        shards, mesh=mesh, in_specs=(field, field, P("diag", "bins"), whole, whole, whole, whole),
        out_specs=(field, field, whole, whole, whole), check_vma=False)
```

```python
import jax
import jax.numpy as jnp
from jax import lax
from jax.experimental import pallas as pl
from jax.experimental.pallas import tpu as pltpu
from jax.sharding import PartitionSpec as P

F32, BF16 = jnp.float32, jnp.bfloat16
MESH = pl.DeviceIdType.MESH
C = 32
ROWS = 96
LANES = 128
HALO = 16
STRIP = 8
EXT = ROWS + 2 * HALO
CHUNKS = ROWS // HALO
NEAR = 8
GROUP = 16
PART_ROWS = 10
CELLS = 3145728
PAD = 2 * HALO
LAGS = (-2, -1, 0, 1, 2)
ORDER = sorted(range(1, GROUP), key=lambda step: abs(step - GROUP // 2))
TAPS = [(a, b) for a in (-1, 0, 1) for b in (-1, 0, 1)]
SIDE = [(a, b) for a, b in TAPS if a]
CENTER = [(a, b) for a, b in TAPS if not a]
STEP = 4


def sigmoid(v):
    return 0.5 + 0.5 * jnp.tanh(0.5 * v)


def kernel(
    rate, feat_in, cot_in, mask_in, w1_in, b1_in, w2_in,
    out, gfeat, g1, gb, g2,
    feat, cot, mask, w1, b1, w2, c0, c1, c2, c3, strips, s0, s1, s2, s3, s4, s5, s6, s7, maskf, w_side, w_center, bias, conv, conv_back,
    got_d, got_i, got_c, sums, got, part, total, load,
    send_d, recv_d, send_i, recv_i, send_c, recv_c, send1, recv1, send2, recv2, send3, recv3,
):
    center, side = (c0, c1, c2, c3), ((s0, s1), (s2, s3), (s4, s5), (s6, s7))
    bins, diag = lax.axis_index("bins"), lax.axis_index("diag")
    count = lax.axis_size("bins")
    right, left = (bins + 1) % count, (bins + count - 1) % count
    across = 1 - diag
    near, far = (bins % NEAR) * 2 + diag, bins // NEAR

    def near_peer(step):
        rank = (near + step) % GROUP
        return rank, (far * NEAR + rank // 2, rank % 2)

    def far_peer(step):
        rank = (far + step) % GROUP
        return rank, (rank * NEAR + bins % NEAR, diag)

    peers = [far_peer(s)[1] for s in ORDER] + [near_peer(s)[1] for s in ORDER]
    peers += [(left, diag), (right, diag), (left, across), (right, across)]
    barrier = pltpu.get_barrier_semaphore()
    for peer in peers:
        pl.semaphore_signal(barrier, inc=1, device_id=peer, device_id_type=MESH)

    r1, r2 = rate[0], rate[1]
    lane = lax.broadcasted_iota(jnp.int32, (C, LANES), 1)
    edge_start = (ROWS - HALO) * (1 - diag)
    edge_chunk = (CHUNKS - 1) * (1 - diag)
    halo_start = (ROWS + HALO) * (1 - diag)
    zero_start = (ROWS + HALO) * diag

    edge = pl.ds(pl.multiple_of(edge_start, HALO), HALO)
    rest = pl.ds(pl.multiple_of(HALO * diag, HALO), ROWS - HALO)
    loads = [
        pltpu.make_async_copy(src, dst, load.at[k])
        for k, (src, dst) in enumerate((
            (mask_in, mask),
            (feat_in.at[:, edge], feat.at[:, edge]),
            (cot_in.at[:, edge], cot.at[:, edge]),
            (feat_in.at[:, rest], feat.at[:, rest]),
            (cot_in.at[:, rest], cot.at[:, rest]),
            (w1_in, w1),
            (w2_in, w2),
            (b1_in, b1),
        ))
    ]
    for copy in loads:
        copy.start()
    for field in range(4):
        center[field][:PAD] = jnp.zeros((PAD, C, LANES), BF16)
        center[field][PAD + ROWS :] = jnp.zeros((PAD, C, LANES), BF16)
        for k in range(2):
            side[field][k][pl.ds(zero_start, HALO)] = jnp.zeros((HALO, C, LANES), BF16)
    loads[0].wait()
    maskf[...] = mask[...].astype(F32)

    def enter(q):
        rows = pl.ds(pl.multiple_of(q * HALO, HALO), HALO)
        m = maskf[rows, :][None]
        x = feat[:, rows, :].astype(F32)
        inner = pl.ds(pl.multiple_of(PAD + q * HALO, HALO), HALO)
        center[0][inner] = jnp.transpose((x * sigmoid(x) * m).astype(BF16), (1, 0, 2))
        grad = (cot[:, rows, :].astype(F32) * m).astype(BF16)
        center[1][inner] = jnp.transpose(grad, (1, 0, 2))

    def row_of(field, d):
        return center[field][PAD + d]

    def strip_copy(rnd, side, q):
        return pltpu.make_async_remote_copy(
            src_ref=strips.at[rnd, side, q], dst_ref=got_i.at[rnd, side, q],
            send_sem=send_i.at[rnd, side, q], recv_sem=recv_i.at[rnd, side, q],
            device_id=((right, left)[side], diag), device_id_type=MESH)

    def corner_copy(rnd, side):
        return pltpu.make_async_remote_copy(
            src_ref=strips.at[rnd, side, edge_chunk], dst_ref=got_c.at[rnd, side],
            send_sem=send_c.at[rnd, side], recv_sem=recv_c.at[rnd, side],
            device_id=((right, left)[side], across), device_id_type=MESH)

    def pack(rnd, q):
        for slot in range(2):
            up = jnp.zeros((C, LANES), BF16)
            down = jnp.zeros((C, LANES), BF16)
            for j in range(HALO):
                row = row_of(2 * rnd + slot, q * HALO + j)
                inside = (lane >= STRIP * j) & (lane < STRIP * (j + 1))
                up = jnp.where(inside, pltpu.roll(row, (STRIP * (j + 1)) % LANES, 1), up)
                down = jnp.where(inside, pltpu.roll(row, STRIP * j, 1), down)
            strips[rnd, 0, q, slot] = up
            strips[rnd, 1, q, slot] = down

    def order(n):
        return n + diag * (CHUNKS - 1 - 2 * n)

    def edge_copy(field):
        rnd, slot = field // 2, field % 2
        return pltpu.make_async_remote_copy(
            src_ref=center[field].at[pl.ds(PAD + edge_start, HALO)], dst_ref=got_d.at[rnd, slot],
            send_sem=send_d.at[rnd, slot], recv_sem=recv_d.at[rnd, slot],
            device_id=(bins, across), device_id_type=MESH)

    def settle(rnd, q):
        for side, end in ((0, 0), (1, count - 1)):
            strip_copy(rnd, side, q).wait_recv()

            @pl.when(bins == end)
            def _():
                got_i[rnd, side, q] = jnp.zeros((2, C, LANES), BF16)

    def settle_halo(rnd):
        edge_copy(2 * rnd).wait_recv()
        edge_copy(2 * rnd + 1).wait_recv()
        for side, end in ((0, 0), (1, count - 1)):
            corner_copy(rnd, side).wait_recv()

            @pl.when(bins == end)
            def _():
                got_c[rnd, side] = jnp.zeros((2, C, LANES), BF16)

    def shift_rows(row_of, before, after, r, store, which):
        for j in which:
            row = row_of(j)
            low = pltpu.roll(before, (r - STRIP * (j + 1) + LANES) % LANES, 1)
            high = pltpu.roll(after, (2 * LANES - r - STRIP * j) % LANES, 1)
            store(j, 0, jnp.where(lane < r, low, pltpu.roll(row, r, 1)))
            store(j, 1, jnp.where(lane >= LANES - r, high, pltpu.roll(row, LANES - r, 1)))

    def shift(rnd, q, rates, which=range(HALO)):
        for slot in range(2):
            field = 2 * rnd + slot

            def store(j, k, value):
                side[field][k][HALO + q * HALO + j] = value

            shift_rows(lambda j: row_of(field, q * HALO + j), got_i[rnd, 0, q, slot],
                       got_i[rnd, 1, q, slot], rates[slot], store, which)

    def shift_halo(rnd, rates, which=range(HALO)):
        for slot in range(2):
            field = 2 * rnd + slot

            def store(j, k, value):
                side[field][k][halo_start + j] = value

            rows = got_d.at[rnd, slot]
            for j in which:
                center[field][HALO + halo_start + j] = rows[j]
            shift_rows(lambda j: rows[j], got_c[rnd, 0, slot], got_c[rnd, 1, slot], rates[slot], store, which)

    def patches(taps, field, r, sign, d):
        blocks = []
        for a, b in taps:
            start = HALO + d + sign * (b - a) * r
            if a:
                rows = [side[field][(sign * a + 1) // 2][start + j] for j in range(STEP)]
            else:
                rows = [center[field][HALO + start + j] for j in range(STEP)]
            blocks.append(jnp.concatenate(rows, axis=1))
        return jnp.concatenate(blocks, axis=0)

    def apply(weight, *which):
        taps = [w_center[weight] if w == 0 else w_side[weight] for w in which]
        return taps[0] if len(taps) == 1 else jnp.concatenate(taps, axis=1)

    loads[1].wait()
    loads[2].wait()
    enter(edge_chunk)
    pack(0, edge_chunk)
    loads[3].wait()
    loads[4].wait()

    def enter_more(n, _):
        enter(order(n))
        pack(0, order(n))
        return 0

    ahead = 3
    lax.fori_loop(0, ahead, enter_more, 0)
    pl.semaphore_wait(barrier, len(peers))
    def strips_out(rnd, q):
        for k in range(2):
            strip_copy(rnd, k, q).start()

    def corners_out(rnd):
        for k in range(2):
            corner_copy(rnd, k).start()

    def first_strips(n, _):
        strips_out(0, order(n))
        return 0

    corners_out(0)
    lax.fori_loop(0, ahead, first_strips, 0)
    strips_out(0, edge_chunk)
    edge_copy(0).start()

    def enter_rest(n, _):
        enter_more(n, 0)
        strips_out(0, order(n))
        return 0

    lax.fori_loop(ahead, CHUNKS - 1, enter_rest, 0)
    edge_copy(1).start()

    for copy in loads[5:]:
        copy.wait()
    bias[...] = jnp.broadcast_to(jnp.transpose(jnp.broadcast_to(b1[...], (C, C)))[:, :1], (C, LANES))
    for k, ref in enumerate((w1, w2)):
        taps = [ref[t] for t in range(9)]
        turned = [jnp.transpose(t.astype(F32)).astype(BF16) for t in taps]
        for m, blocks in ((2 * k, taps), (2 * k + 1, turned)):
            w_side[m] = jnp.concatenate(blocks[:3] + blocks[6:], axis=1)
            w_center[m] = jnp.concatenate(blocks[3:6], axis=1)

    def middle_center(q):
        for step in range(HALO // STEP):
            d = q * HALO + step * STEP
            pre = jnp.dot(w_center[0], patches(CENTER, 0, r1, 1, d), preferred_element_type=F32)
            back = jnp.dot(w_center[3], patches(CENTER, 1, r2, -1, d), preferred_element_type=F32)
            for j in range(STEP):
                conv[d + j] = pre[:, j * LANES : (j + 1) * LANES] + bias[...]
                conv_back[d + j] = back[:, j * LANES : (j + 1) * LANES]

    def middle(d):
        pre = jnp.dot(w_side[0], patches(SIDE, 0, r1, 1, d), preferred_element_type=F32)
        back = jnp.dot(w_side[3], patches(SIDE, 1, r2, -1, d), preferred_element_type=F32)
        for j in range(STEP):
            m = maskf[pl.ds(d + j, 1), :]
            y = pre[:, j * LANES : (j + 1) * LANES] + conv[d + j]
            s = sigmoid(y)
            center[2][PAD + d + j] = (y * s * m).astype(BF16)
            grad = back[:, j * LANES : (j + 1) * LANES] + conv_back[d + j]
            center[3][PAD + d + j] = (grad * m * (s * (1.0 + y * (1.0 - s)))).astype(BF16)

    def center_step(n, _):
        middle_center(order(n))
        return 0

    lax.fori_loop(0, CHUNKS - 1, center_step, 0)

    def middle_chunk(q, beside=None):
        for step in range(HALO // STEP):
            middle(q * HALO + step * STEP)
            if beside is not None:
                beside(range(step * STEP, step * STEP + STEP))

    for n in range(2):
        settle(0, order(n))
        shift(0, order(n), (r1, r2))

    def middle_step(n, _):
        settle(0, order(n + 2))
        middle_chunk(order(n), lambda which: shift(0, order(n + 2), (r1, r2), which))
        return 0

    lax.fori_loop(0, CHUNKS - 2, middle_step, 0)
    settle_halo(0)
    middle_chunk(order(CHUNKS - 2), lambda which: shift_halo(0, (r1, r2), which))
    middle_center(edge_chunk)
    middle_chunk(edge_chunk)
    edge_copy(2).start()

    wide = 28
    nt = (((1,), (1,)), ((), ()))

    def row_block(rows):
        return jnp.concatenate(rows, axis=1)

    def near_rows(field, k):
        before = row_block([side[field][0][k + j] for j in range(wide)])
        same = row_block([center[field][HALO + k + j] for j in range(wide)])
        return [before, same, row_block([side[field][1][k + j] for j in range(wide)])]

    def grads(n, carry):
        k = n * wide + HALO * (1 - diag)
        act = near_rows(0, k)
        act.append(jnp.ones((C, wide * LANES), BF16))
        ups = [row_block([center[3][HALO + k - m * r1 + j] for j in range(wide)]) for m in LAGS]
        one = lax.dot_general(jnp.concatenate(ups, axis=0), jnp.concatenate(act, axis=0), nt,
                              preferred_element_type=F32)
        grad = near_rows(1, k)
        hid = [row_block([center[2][HALO + k + m * r2 + j] for j in range(wide)]) for m in LAGS]
        two = lax.dot_general(jnp.concatenate(grad, axis=0), jnp.concatenate(hid, axis=0), nt,
                              preferred_element_type=F32)
        return carry[0] + one, carry[1] + two

    zero = (jnp.zeros((5 * C, 4 * C), F32), jnp.zeros((3 * C, 5 * C), F32))
    one, two = lax.fori_loop(0, (EXT - HALO) // wide, grads, zero, unroll=2)

    def block(value, i, j):
        return value[C * i : C * (i + 1), C * j : C * (j + 1)]

    blocks = [[block(one, b - a + 2, a + 1) for a, b in TAPS], [block(two, 1 - a, b - a + 2) for a, b in TAPS]]
    rows = [jnp.concatenate(blocks[k][4 * p : 4 * p + 4], axis=1) for k in range(2) for p in range(2)]
    rows.append(jnp.concatenate([blocks[0][8], blocks[1][8], block(one, 2, 3), jnp.zeros((C, C), F32)], axis=1))
    rows = jnp.concatenate(rows, axis=0)
    for k in range(GROUP):
        sums[k] = rows[PART_ROWS * k : PART_ROWS * (k + 1)]

    def scatter(step):
        rank, device = near_peer(step)
        return rank, pltpu.make_async_remote_copy(
            src_ref=sums.at[rank], dst_ref=got.at[step], send_sem=send1.at[step],
            recv_sem=recv1.at[step], device_id=device, device_id_type=MESH)

    for step in ORDER:
        scatter(step)[1].start()
    edge_copy(3).start()

    pack(1, edge_chunk)
    strips_out(1, edge_chunk)
    corners_out(1)

    def launch_rest(n, _):
        pack(1, order(n))
        strips_out(1, order(n))
        return 0

    lax.fori_loop(0, CHUNKS - 1, launch_rest, 0)

    spread = []
    for step in ORDER:
        rank, device = far_peer(step)
        spread.append(pltpu.make_async_remote_copy(
            src_ref=part.at[far], dst_ref=part.at[far], send_sem=send2.at[step],
            recv_sem=recv2.at[step], device_id=device, device_id_type=MESH))

    value = sums[near]
    for step in ORDER:
        scatter(step)[1].wait_recv()
        value = value + got[step]
    part[far] = value
    for copy in spread:
        copy.start()

    def last_conv(weight, field, r, sign, q, beside=None):
        for step in range(HALO // STEP):
            d = q * HALO + step * STEP
            taps = patches(SIDE + CENTER, field, r, sign, d)
            y = jnp.dot(apply(weight, 1, 0), taps, preferred_element_type=F32)
            for j in range(STEP):
                conv[d + j] = y[:, j * LANES : (j + 1) * LANES]
            if beside is not None:
                beside(range(step * STEP, step * STEP + STEP))

    for n in range(2):
        settle(1, order(n))
        shift(1, order(n), (r2, r1))

    def forward(n, _):
        settle(1, order(n + 2))
        last_conv(2, 2, r2, 1, order(n), lambda which: shift(1, order(n + 2), (r2, r1), which))
        return 0

    lax.fori_loop(0, CHUNKS - 2, forward, 0)
    settle_halo(1)
    last_conv(2, 2, r2, 1, order(CHUNKS - 2), lambda which: shift_halo(1, (r2, r1), which))
    last_conv(2, 2, r2, 1, edge_chunk)

    def finish_forward(q, _):
        rows = pl.ds(pl.multiple_of(q * HALO, HALO), HALO)
        y = jnp.transpose(conv[rows], (1, 0, 2))
        out[:, rows, :] = (feat[:, rows, :].astype(F32) + maskf[rows, :][None] * y).astype(BF16)
        return 0

    lax.fori_loop(0, CHUNKS, finish_forward, 0)
    def gather(step):
        return near_peer(step)[0], pltpu.make_async_remote_copy(
            src_ref=total.at[near], dst_ref=total.at[near], send_sem=send3.at[step],
            recv_sem=recv3.at[step], device_id=near_peer(step)[1], device_id_type=MESH)

    for copy in spread:
        copy.wait_recv()
    value = part[0]
    for rank in range(1, GROUP):
        value = value + part[rank]
    total[near] = value
    for step in ORDER:
        gather(step)[1].start()

    def backward(q, _):
        last_conv(1, 3, r1, -1, q)
        return 0

    lax.fori_loop(0, CHUNKS, backward, 0)

    def finish_backward(q, _):
        rows = pl.ds(pl.multiple_of(q * HALO, HALO), HALO)
        y = jnp.transpose(conv[rows], (1, 0, 2))
        x = feat[:, rows, :].astype(F32)
        s = sigmoid(x)
        slope = maskf[rows, :][None] * (s * (1.0 + x * (1.0 - s)))
        gfeat[:, rows, :] = (cot[:, rows, :].astype(F32) + slope * y).astype(BF16)
        return 0

    lax.fori_loop(0, CHUNKS, finish_backward, 0)
    for field in range(4):
        edge_copy(field).wait_send()

    def sent(q, _):
        for rnd in range(2):
            for side in range(2):
                strip_copy(rnd, side, q).wait_send()
        return 0

    lax.fori_loop(0, CHUNKS, sent, 0)
    for rnd in range(2):
        for way in range(2):
            corner_copy(rnd, way).wait_send()
    for step in ORDER:
        scatter(step)[1].wait_send()
    for copy in spread:
        copy.wait_send()
    for step in ORDER:
        gather(step)[1].wait()

    factor = 1.0 / jnp.sqrt(jnp.float32(CELLS))
    rows = jnp.concatenate([total[k] for k in range(GROUP)], axis=0) * factor
    last = rows[4 * C :]
    for k, ref in enumerate((g1, g2)):
        for t in range(8):
            base = C * (2 * k + t // 4)
            ref[t] = rows[base : base + C, C * (t % 4) : C * (t % 4 + 1)]
        ref[8] = last[:, C * k : C * (k + 1)]
    gb[...] = jnp.transpose(last[:, 2 * C : 3 * C])[:1]


def hand_over(*refs):
    given, results, sems = refs[:5], refs[5:10], refs[10]
    copies = [pltpu.make_async_copy(given[k], results[k], sems.at[k]) for k in range(5)]
    for copy in copies:
        copy.start()
    for copy in copies:
        copy.wait()


def shards(features, cotangent, band_mask, dilation, w_first, b_first, w_second):
    vmem = pl.BlockSpec(memory_space=pltpu.VMEM)
    dma = pltpu.SemaphoreType.DMA
    shape = jax.ShapeDtypeStruct
    field = (C, ROWS, LANES)
    taps = (9, C, C)
    hbm = pl.BlockSpec(memory_space=pltpu.HBM)
    results = pl.pallas_call(
        kernel,
        out_shape=[pltpu.VMEM(field, BF16), pltpu.VMEM(field, BF16), pltpu.VMEM(taps, F32), pltpu.VMEM((1, C), F32), pltpu.VMEM(taps, F32)],
        in_specs=[pl.BlockSpec(memory_space=pltpu.SMEM)] + [hbm] * 6,
        out_specs=[vmem] * 5,
        scratch_shapes=[
            pltpu.VMEM(field, BF16),
            pltpu.VMEM(field, BF16),
            pltpu.VMEM((ROWS, LANES), jnp.int32),
            pltpu.VMEM(taps, BF16),
            pltpu.VMEM((1, C), F32),
            pltpu.VMEM(taps, BF16),
            pltpu.VMEM((ROWS + 2 * PAD, C, LANES), BF16),
            pltpu.VMEM((ROWS + 2 * PAD, C, LANES), BF16),
            pltpu.VMEM((ROWS + 2 * PAD, C, LANES), BF16),
            pltpu.VMEM((ROWS + 2 * PAD, C, LANES), BF16),
            pltpu.VMEM((2, 2, CHUNKS, 2, C, LANES), BF16),
            pltpu.VMEM((EXT, C, LANES), BF16),
            pltpu.VMEM((EXT, C, LANES), BF16),
            pltpu.VMEM((EXT, C, LANES), BF16),
            pltpu.VMEM((EXT, C, LANES), BF16),
            pltpu.VMEM((EXT, C, LANES), BF16),
            pltpu.VMEM((EXT, C, LANES), BF16),
            pltpu.VMEM((EXT, C, LANES), BF16),
            pltpu.VMEM((EXT, C, LANES), BF16),
            pltpu.VMEM((ROWS, LANES), F32),
            pltpu.VMEM((4, C, 6 * C), BF16),
            pltpu.VMEM((4, C, 3 * C), BF16),
            pltpu.VMEM((C, LANES), F32),
            pltpu.VMEM((ROWS, C, LANES), F32),
            pltpu.VMEM((ROWS, C, LANES), F32),
            pltpu.VMEM((2, 2, HALO, C, LANES), BF16),
            pltpu.VMEM((2, 2, CHUNKS, 2, C, LANES), BF16),
            pltpu.VMEM((2, 2, 2, C, LANES), BF16),
            pltpu.VMEM((GROUP, PART_ROWS, LANES), F32),
            pltpu.VMEM((GROUP, PART_ROWS, LANES), F32),
            pltpu.VMEM((GROUP, PART_ROWS, LANES), F32),
            pltpu.VMEM((GROUP, PART_ROWS, LANES), F32),
            dma((8,)),
            dma((2, 2)), dma((2, 2)), dma((2, 2, CHUNKS)), dma((2, 2, CHUNKS)), dma((2, 2)), dma((2, 2)),
            dma((GROUP,)), dma((GROUP,)), dma((GROUP,)), dma((GROUP,)), dma((GROUP,)), dma((GROUP,)),
        ],
        compiler_params=pltpu.CompilerParams(
            collective_id=0, has_side_effects=True, vmem_limit_bytes=61 * 1024 * 1024
        ),
    )(dilation, features, cotangent, band_mask, jnp.transpose(w_first, (1, 0, 2)), b_first[None],
      jnp.transpose(w_second, (1, 0, 2)))
    out, gfeat, g1, gb, g2 = pl.pallas_call(
        hand_over,
        out_shape=[shape(r.shape, r.dtype) for r in results],
        in_specs=[vmem] * 5,
        out_specs=[hbm] * 5,
        scratch_shapes=[dma((5,))],
        compiler_params=pltpu.CompilerParams(vmem_limit_bytes=8 * 1024 * 1024),
    )(*results)
    return (out, gfeat, jnp.transpose(g1, (1, 0, 2)), gb[0], jnp.transpose(g2, (1, 0, 2)))


def solution(mesh):
    field, whole = P(None, "diag", "bins"), P()
    return jax.shard_map(
        shards, mesh=mesh, in_specs=(field, field, P("diag", "bins"), whole, whole, whole, whole),
        out_specs=(field, field, whole, whole, whole), check_vma=False)
```

```python
import jax
import jax.numpy as jnp
from jax import lax
from jax.experimental import pallas as pl
from jax.experimental.pallas import tpu as pltpu
from jax.sharding import PartitionSpec as P

F32, BF16 = jnp.float32, jnp.bfloat16
MESH = pl.DeviceIdType.MESH
C = 32
ROWS = 96
LANES = 128
HALO = 16
STRIP = 8
EXT = ROWS + 2 * HALO
CHUNKS = ROWS // HALO
NEAR = 8
GROUP = 16
PART_ROWS = 10
CELLS = 3145728
PAD = 2 * HALO
LAGS = (-2, -1, 0, 1, 2)
ORDER = sorted(range(1, GROUP), key=lambda step: abs(step - GROUP // 2))
TAPS = [(a, b) for a in (-1, 0, 1) for b in (-1, 0, 1)]
SIDE = [(a, b) for a, b in TAPS if a]
CENTER = [(a, b) for a, b in TAPS if not a]
STEP = 4


def sigmoid(v):
    return 0.5 + 0.5 * jnp.tanh(0.5 * v)


def kernel(
    rate, feat_in, cot_in, mask_in, w1_in, b1_in, w2_in,
    out, gfeat, g1, gb, g2,
    feat, cot, mask, w1, b1, w2, c0, c1, c2, c3, strips, s0, s1, s2, s3, s4, s5, s6, s7, maskf, w_side, w_center, bias, conv, conv_back,
    got_d, got_i, got_c, sums, got, part, total, load,
    send_d, recv_d, send_i, recv_i, send_c, recv_c, send1, recv1, send2, recv2, send3, recv3,
):
    center, side = (c0, c1, c2, c3), ((s0, s1), (s2, s3), (s4, s5), (s6, s7))
    bins, diag = lax.axis_index("bins"), lax.axis_index("diag")
    count = lax.axis_size("bins")
    right, left = (bins + 1) % count, (bins + count - 1) % count
    across = 1 - diag
    near, far = (bins % NEAR) * 2 + diag, bins // NEAR

    def near_peer(step):
        rank = (near + step) % GROUP
        return rank, (far * NEAR + rank // 2, rank % 2)

    def far_peer(step):
        rank = (far + step) % GROUP
        return rank, (rank * NEAR + bins % NEAR, diag)

    peers = [far_peer(s)[1] for s in ORDER] + [near_peer(s)[1] for s in ORDER]
    peers += [(left, diag), (right, diag), (left, across), (right, across)]
    barrier = pltpu.get_barrier_semaphore()
    for peer in peers:
        pl.semaphore_signal(barrier, inc=1, device_id=peer, device_id_type=MESH)

    r1, r2 = rate[0], rate[1]
    lane = lax.broadcasted_iota(jnp.int32, (C, LANES), 1)
    edge_start = (ROWS - HALO) * (1 - diag)
    edge_chunk = (CHUNKS - 1) * (1 - diag)
    halo_start = (ROWS + HALO) * (1 - diag)
    zero_start = (ROWS + HALO) * diag

    edge = pl.ds(pl.multiple_of(edge_start, HALO), HALO)
    rest = pl.ds(pl.multiple_of(HALO * diag, HALO), ROWS - HALO)
    loads = [
        pltpu.make_async_copy(src, dst, load.at[k])
        for k, (src, dst) in enumerate((
            (mask_in, mask),
            (feat_in.at[:, edge], feat.at[:, edge]),
            (cot_in.at[:, edge], cot.at[:, edge]),
            (feat_in.at[:, rest], feat.at[:, rest]),
            (cot_in.at[:, rest], cot.at[:, rest]),
            (w1_in, w1),
            (w2_in, w2),
            (b1_in, b1),
        ))
    ]
    for copy in loads:
        copy.start()
    for field in range(4):
        center[field][:PAD] = jnp.zeros((PAD, C, LANES), BF16)
        center[field][PAD + ROWS :] = jnp.zeros((PAD, C, LANES), BF16)
        for k in range(2):
            side[field][k][pl.ds(zero_start, HALO)] = jnp.zeros((HALO, C, LANES), BF16)
    loads[0].wait()
    maskf[...] = mask[...].astype(F32)

    def enter(q):
        rows = pl.ds(pl.multiple_of(q * HALO, HALO), HALO)
        m = maskf[rows, :][None]
        x = feat[:, rows, :].astype(F32)
        inner = pl.ds(pl.multiple_of(PAD + q * HALO, HALO), HALO)
        center[0][inner] = jnp.transpose((x * sigmoid(x) * m).astype(BF16), (1, 0, 2))
        grad = (cot[:, rows, :].astype(F32) * m).astype(BF16)
        center[1][inner] = jnp.transpose(grad, (1, 0, 2))

    def row_of(field, d):
        return center[field][PAD + d]

    def strip_copy(rnd, side, q):
        return pltpu.make_async_remote_copy(
            src_ref=strips.at[rnd, side, q], dst_ref=got_i.at[rnd, side, q],
            send_sem=send_i.at[rnd, side, q], recv_sem=recv_i.at[rnd, side, q],
            device_id=((right, left)[side], diag), device_id_type=MESH)

    def corner_copy(rnd, side):
        return pltpu.make_async_remote_copy(
            src_ref=strips.at[rnd, side, edge_chunk], dst_ref=got_c.at[rnd, side],
            send_sem=send_c.at[rnd, side], recv_sem=recv_c.at[rnd, side],
            device_id=((right, left)[side], across), device_id_type=MESH)

    def pack(rnd, q):
        for slot in range(2):
            up = jnp.zeros((C, LANES), BF16)
            down = jnp.zeros((C, LANES), BF16)
            for j in range(HALO):
                row = row_of(2 * rnd + slot, q * HALO + j)
                inside = (lane >= STRIP * j) & (lane < STRIP * (j + 1))
                up = jnp.where(inside, pltpu.roll(row, (STRIP * (j + 1)) % LANES, 1), up)
                down = jnp.where(inside, pltpu.roll(row, STRIP * j, 1), down)
            strips[rnd, 0, q, slot] = up
            strips[rnd, 1, q, slot] = down

    def order(n):
        return n + diag * (CHUNKS - 1 - 2 * n)

    def edge_copy(field):
        rnd, slot = field // 2, field % 2
        return pltpu.make_async_remote_copy(
            src_ref=center[field].at[pl.ds(PAD + edge_start, HALO)], dst_ref=got_d.at[rnd, slot],
            send_sem=send_d.at[rnd, slot], recv_sem=recv_d.at[rnd, slot],
            device_id=(bins, across), device_id_type=MESH)

    def settle(rnd, q):
        for side, end in ((0, 0), (1, count - 1)):
            strip_copy(rnd, side, q).wait_recv()

            @pl.when(bins == end)
            def _():
                got_i[rnd, side, q] = jnp.zeros((2, C, LANES), BF16)

    def settle_halo(rnd):
        edge_copy(2 * rnd).wait_recv()
        edge_copy(2 * rnd + 1).wait_recv()
        for side, end in ((0, 0), (1, count - 1)):
            corner_copy(rnd, side).wait_recv()

            @pl.when(bins == end)
            def _():
                got_c[rnd, side] = jnp.zeros((2, C, LANES), BF16)

    def shift_rows(row_of, before, after, r, store, which):
        for j in which:
            row = row_of(j)
            low = pltpu.roll(before, (r - STRIP * (j + 1) + LANES) % LANES, 1)
            high = pltpu.roll(after, (2 * LANES - r - STRIP * j) % LANES, 1)
            store(j, 0, jnp.where(lane < r, low, pltpu.roll(row, r, 1)))
            store(j, 1, jnp.where(lane >= LANES - r, high, pltpu.roll(row, LANES - r, 1)))

    def shift(rnd, q, rates, which=range(HALO)):
        for slot in range(2):
            field = 2 * rnd + slot

            def store(j, k, value):
                side[field][k][HALO + q * HALO + j] = value

            shift_rows(lambda j: row_of(field, q * HALO + j), got_i[rnd, 0, q, slot],
                       got_i[rnd, 1, q, slot], rates[slot], store, which)

    def shift_halo(rnd, rates, which=range(HALO)):
        for slot in range(2):
            field = 2 * rnd + slot

            def store(j, k, value):
                side[field][k][halo_start + j] = value

            rows = got_d.at[rnd, slot]
            for j in which:
                center[field][HALO + halo_start + j] = rows[j]
            shift_rows(lambda j: rows[j], got_c[rnd, 0, slot], got_c[rnd, 1, slot], rates[slot], store, which)

    def patches(taps, field, r, sign, d):
        blocks = []
        for a, b in taps:
            start = HALO + d + sign * (b - a) * r
            if a:
                rows = [side[field][(sign * a + 1) // 2][start + j] for j in range(STEP)]
            else:
                rows = [center[field][HALO + start + j] for j in range(STEP)]
            blocks.append(jnp.concatenate(rows, axis=1))
        return jnp.concatenate(blocks, axis=0)

    def apply(weight, *which):
        taps = [w_center[weight] if w == 0 else w_side[weight] for w in which]
        return taps[0] if len(taps) == 1 else jnp.concatenate(taps, axis=1)

    loads[1].wait()
    loads[2].wait()
    enter(edge_chunk)
    pack(0, edge_chunk)
    loads[3].wait()
    loads[4].wait()

    def enter_more(n, _):
        enter(order(n))
        pack(0, order(n))
        return 0

    ahead = 5
    lax.fori_loop(0, ahead, enter_more, 0)
    pl.semaphore_wait(barrier, len(peers))
    def strips_out(rnd, q):
        for k in range(2):
            strip_copy(rnd, k, q).start()

    def corners_out(rnd):
        for k in range(2):
            corner_copy(rnd, k).start()

    def first_strips(n, _):
        strips_out(0, order(n))
        return 0

    corners_out(0)
    lax.fori_loop(0, ahead, first_strips, 0)
    strips_out(0, edge_chunk)
    edge_copy(0).start()

    def enter_rest(n, _):
        enter_more(n, 0)
        strips_out(0, order(n))
        return 0

    lax.fori_loop(ahead, CHUNKS - 1, enter_rest, 0)
    edge_copy(1).start()

    for copy in loads[5:]:
        copy.wait()
    bias[...] = jnp.broadcast_to(jnp.transpose(jnp.broadcast_to(b1[...], (C, C)))[:, :1], (C, LANES))
    for k, ref in enumerate((w1, w2)):
        taps = [ref[t] for t in range(9)]
        turned = [jnp.transpose(t.astype(F32)).astype(BF16) for t in taps]
        for m, blocks in ((2 * k, taps), (2 * k + 1, turned)):
            w_side[m] = jnp.concatenate(blocks[:3] + blocks[6:], axis=1)
            w_center[m] = jnp.concatenate(blocks[3:6], axis=1)

    def middle_center(q):
        for step in range(HALO // STEP):
            d = q * HALO + step * STEP
            pre = jnp.dot(w_center[0], patches(CENTER, 0, r1, 1, d), preferred_element_type=F32)
            back = jnp.dot(w_center[3], patches(CENTER, 1, r2, -1, d), preferred_element_type=F32)
            for j in range(STEP):
                conv[d + j] = pre[:, j * LANES : (j + 1) * LANES] + bias[...]
                conv_back[d + j] = back[:, j * LANES : (j + 1) * LANES]

    def middle(d):
        pre = jnp.dot(w_side[0], patches(SIDE, 0, r1, 1, d), preferred_element_type=F32)
        back = jnp.dot(w_side[3], patches(SIDE, 1, r2, -1, d), preferred_element_type=F32)
        for j in range(STEP):
            m = maskf[pl.ds(d + j, 1), :]
            y = pre[:, j * LANES : (j + 1) * LANES] + conv[d + j]
            s = sigmoid(y)
            center[2][PAD + d + j] = (y * s * m).astype(BF16)
            grad = back[:, j * LANES : (j + 1) * LANES] + conv_back[d + j]
            center[3][PAD + d + j] = (grad * m * (s * (1.0 + y * (1.0 - s)))).astype(BF16)

    def center_step(n, _):
        middle_center(order(n))
        return 0

    lax.fori_loop(0, CHUNKS - 1, center_step, 0)

    def middle_chunk(q, beside=None):
        for step in range(HALO // STEP):
            middle(q * HALO + step * STEP)
            if beside is not None:
                beside(range(step * STEP, step * STEP + STEP))

    for n in range(2):
        settle(0, order(n))
        shift(0, order(n), (r1, r2))

    def middle_step(n, _):
        settle(0, order(n + 2))
        middle_chunk(order(n), lambda which: shift(0, order(n + 2), (r1, r2), which))
        return 0

    lax.fori_loop(0, CHUNKS - 2, middle_step, 0)
    settle_halo(0)
    middle_chunk(order(CHUNKS - 2), lambda which: shift_halo(0, (r1, r2), which))
    middle_center(edge_chunk)
    middle_chunk(edge_chunk)
    edge_copy(2).start()

    wide = 16
    nt = (((1,), (1,)), ((), ()))

    def row_block(rows):
        return jnp.concatenate(rows, axis=1)

    def near_rows(field, k):
        before = row_block([side[field][0][k + j] for j in range(wide)])
        same = row_block([center[field][HALO + k + j] for j in range(wide)])
        return [before, same, row_block([side[field][1][k + j] for j in range(wide)])]

    def grads(n, carry):
        k = n * wide + HALO * (1 - diag)
        act = near_rows(0, k)
        act.append(jnp.ones((C, wide * LANES), BF16))
        ups = [row_block([center[3][HALO + k - m * r1 + j] for j in range(wide)]) for m in LAGS]
        one = lax.dot_general(jnp.concatenate(ups, axis=0), jnp.concatenate(act, axis=0), nt,
                              preferred_element_type=F32)
        grad = near_rows(1, k)
        hid = [row_block([center[2][HALO + k + m * r2 + j] for j in range(wide)]) for m in LAGS]
        two = lax.dot_general(jnp.concatenate(grad, axis=0), jnp.concatenate(hid, axis=0), nt,
                              preferred_element_type=F32)
        return carry[0] + one, carry[1] + two

    zero = (jnp.zeros((5 * C, 4 * C), F32), jnp.zeros((3 * C, 5 * C), F32))
    one, two = lax.fori_loop(0, (EXT - HALO) // wide, grads, zero, unroll=7)

    def block(value, i, j):
        return value[C * i : C * (i + 1), C * j : C * (j + 1)]

    blocks = [[block(one, b - a + 2, a + 1) for a, b in TAPS], [block(two, 1 - a, b - a + 2) for a, b in TAPS]]
    rows = [jnp.concatenate(blocks[k][4 * p : 4 * p + 4], axis=1) for k in range(2) for p in range(2)]
    rows.append(jnp.concatenate([blocks[0][8], blocks[1][8], block(one, 2, 3), jnp.zeros((C, C), F32)], axis=1))
    rows = jnp.concatenate(rows, axis=0)
    for k in range(GROUP):
        sums[k] = rows[PART_ROWS * k : PART_ROWS * (k + 1)]

    def scatter(step):
        rank, device = near_peer(step)
        return rank, pltpu.make_async_remote_copy(
            src_ref=sums.at[rank], dst_ref=got.at[step], send_sem=send1.at[step],
            recv_sem=recv1.at[step], device_id=device, device_id_type=MESH)

    for step in ORDER:
        scatter(step)[1].start()
    edge_copy(3).start()

    pack(1, edge_chunk)
    strips_out(1, edge_chunk)
    corners_out(1)

    def launch_rest(n, _):
        pack(1, order(n))
        strips_out(1, order(n))
        return 0

    lax.fori_loop(0, CHUNKS - 1, launch_rest, 0)

    spread = []
    for step in ORDER:
        rank, device = far_peer(step)
        spread.append(pltpu.make_async_remote_copy(
            src_ref=part.at[far], dst_ref=part.at[far], send_sem=send2.at[step],
            recv_sem=recv2.at[step], device_id=device, device_id_type=MESH))

    value = sums[near]
    for step in ORDER:
        scatter(step)[1].wait_recv()
        value = value + got[step]
    part[far] = value
    for copy in spread:
        copy.start()

    def last_conv(weight, field, r, sign, q, beside=None):
        for step in range(HALO // STEP):
            d = q * HALO + step * STEP
            taps = patches(SIDE + CENTER, field, r, sign, d)
            y = jnp.dot(apply(weight, 1, 0), taps, preferred_element_type=F32)
            for j in range(STEP):
                conv[d + j] = y[:, j * LANES : (j + 1) * LANES]
            if beside is not None:
                beside(range(step * STEP, step * STEP + STEP))

    for n in range(2):
        settle(1, order(n))
        shift(1, order(n), (r2, r1))

    def forward(n, _):
        settle(1, order(n + 2))
        last_conv(2, 2, r2, 1, order(n), lambda which: shift(1, order(n + 2), (r2, r1), which))
        return 0

    lax.fori_loop(0, CHUNKS - 2, forward, 0)
    settle_halo(1)
    last_conv(2, 2, r2, 1, order(CHUNKS - 2), lambda which: shift_halo(1, (r2, r1), which))
    last_conv(2, 2, r2, 1, edge_chunk)

    def finish_forward(q, _):
        rows = pl.ds(pl.multiple_of(q * HALO, HALO), HALO)
        y = jnp.transpose(conv[rows], (1, 0, 2))
        out[:, rows, :] = (feat[:, rows, :].astype(F32) + maskf[rows, :][None] * y).astype(BF16)
        return 0

    lax.fori_loop(0, CHUNKS, finish_forward, 0)
    def gather(step):
        return near_peer(step)[0], pltpu.make_async_remote_copy(
            src_ref=total.at[near], dst_ref=total.at[near], send_sem=send3.at[step],
            recv_sem=recv3.at[step], device_id=near_peer(step)[1], device_id_type=MESH)

    for copy in spread:
        copy.wait_recv()
    value = part[0]
    for rank in range(1, GROUP):
        value = value + part[rank]
    total[near] = value
    for step in ORDER:
        gather(step)[1].start()

    def backward(q, _):
        last_conv(1, 3, r1, -1, q)
        return 0

    lax.fori_loop(0, CHUNKS, backward, 0)

    def finish_backward(q, _):
        rows = pl.ds(pl.multiple_of(q * HALO, HALO), HALO)
        y = jnp.transpose(conv[rows], (1, 0, 2))
        x = feat[:, rows, :].astype(F32)
        s = sigmoid(x)
        slope = maskf[rows, :][None] * (s * (1.0 + x * (1.0 - s)))
        gfeat[:, rows, :] = (cot[:, rows, :].astype(F32) + slope * y).astype(BF16)
        return 0

    lax.fori_loop(0, CHUNKS, finish_backward, 0)
    for field in range(4):
        edge_copy(field).wait_send()

    def sent(q, _):
        for rnd in range(2):
            for side in range(2):
                strip_copy(rnd, side, q).wait_send()
        return 0

    lax.fori_loop(0, CHUNKS, sent, 0)
    for rnd in range(2):
        for way in range(2):
            corner_copy(rnd, way).wait_send()
    for step in ORDER:
        scatter(step)[1].wait_send()
    for copy in spread:
        copy.wait_send()
    for step in ORDER:
        gather(step)[1].wait()

    factor = 1.0 / jnp.sqrt(jnp.float32(CELLS))
    rows = jnp.concatenate([total[k] for k in range(GROUP)], axis=0) * factor
    last = rows[4 * C :]
    for k, ref in enumerate((g1, g2)):
        for t in range(8):
            base = C * (2 * k + t // 4)
            ref[t] = rows[base : base + C, C * (t % 4) : C * (t % 4 + 1)]
        ref[8] = last[:, C * k : C * (k + 1)]
    gb[...] = jnp.transpose(last[:, 2 * C : 3 * C])[:1]


def hand_over(*refs):
    given, results, sems = refs[:5], refs[5:10], refs[10]
    copies = [pltpu.make_async_copy(given[k], results[k], sems.at[k]) for k in range(5)]
    for copy in copies:
        copy.start()
    for copy in copies:
        copy.wait()


def shards(features, cotangent, band_mask, dilation, w_first, b_first, w_second):
    vmem = pl.BlockSpec(memory_space=pltpu.VMEM)
    dma = pltpu.SemaphoreType.DMA
    shape = jax.ShapeDtypeStruct
    field = (C, ROWS, LANES)
    taps = (9, C, C)
    hbm = pl.BlockSpec(memory_space=pltpu.HBM)
    results = pl.pallas_call(
        kernel,
        out_shape=[pltpu.VMEM(field, BF16), pltpu.VMEM(field, BF16), pltpu.VMEM(taps, F32), pltpu.VMEM((1, C), F32), pltpu.VMEM(taps, F32)],
        in_specs=[pl.BlockSpec(memory_space=pltpu.SMEM)] + [hbm] * 6,
        out_specs=[vmem] * 5,
        scratch_shapes=[
            pltpu.VMEM(field, BF16),
            pltpu.VMEM(field, BF16),
            pltpu.VMEM((ROWS, LANES), jnp.int32),
            pltpu.VMEM(taps, BF16),
            pltpu.VMEM((1, C), F32),
            pltpu.VMEM(taps, BF16),
            pltpu.VMEM((ROWS + 2 * PAD, C, LANES), BF16),
            pltpu.VMEM((ROWS + 2 * PAD, C, LANES), BF16),
            pltpu.VMEM((ROWS + 2 * PAD, C, LANES), BF16),
            pltpu.VMEM((ROWS + 2 * PAD, C, LANES), BF16),
            pltpu.VMEM((2, 2, CHUNKS, 2, C, LANES), BF16),
            pltpu.VMEM((EXT, C, LANES), BF16),
            pltpu.VMEM((EXT, C, LANES), BF16),
            pltpu.VMEM((EXT, C, LANES), BF16),
            pltpu.VMEM((EXT, C, LANES), BF16),
            pltpu.VMEM((EXT, C, LANES), BF16),
            pltpu.VMEM((EXT, C, LANES), BF16),
            pltpu.VMEM((EXT, C, LANES), BF16),
            pltpu.VMEM((EXT, C, LANES), BF16),
            pltpu.VMEM((ROWS, LANES), F32),
            pltpu.VMEM((4, C, 6 * C), BF16),
            pltpu.VMEM((4, C, 3 * C), BF16),
            pltpu.VMEM((C, LANES), F32),
            pltpu.VMEM((ROWS, C, LANES), F32),
            pltpu.VMEM((ROWS, C, LANES), F32),
            pltpu.VMEM((2, 2, HALO, C, LANES), BF16),
            pltpu.VMEM((2, 2, CHUNKS, 2, C, LANES), BF16),
            pltpu.VMEM((2, 2, 2, C, LANES), BF16),
            pltpu.VMEM((GROUP, PART_ROWS, LANES), F32),
            pltpu.VMEM((GROUP, PART_ROWS, LANES), F32),
            pltpu.VMEM((GROUP, PART_ROWS, LANES), F32),
            pltpu.VMEM((GROUP, PART_ROWS, LANES), F32),
            dma((8,)),
            dma((2, 2)), dma((2, 2)), dma((2, 2, CHUNKS)), dma((2, 2, CHUNKS)), dma((2, 2)), dma((2, 2)),
            dma((GROUP,)), dma((GROUP,)), dma((GROUP,)), dma((GROUP,)), dma((GROUP,)), dma((GROUP,)),
        ],
        compiler_params=pltpu.CompilerParams(
            collective_id=0, has_side_effects=True, vmem_limit_bytes=61 * 1024 * 1024
        ),
    )(dilation, features, cotangent, band_mask, jnp.transpose(w_first, (1, 0, 2)), b_first[None],
      jnp.transpose(w_second, (1, 0, 2)))
    out, gfeat, g1, gb, g2 = pl.pallas_call(
        hand_over,
        out_shape=[shape(r.shape, r.dtype) for r in results],
        in_specs=[vmem] * 5,
        out_specs=[hbm] * 5,
        scratch_shapes=[dma((5,))],
        compiler_params=pltpu.CompilerParams(vmem_limit_bytes=8 * 1024 * 1024),
    )(*results)
    return (out, gfeat, jnp.transpose(g1, (1, 0, 2)), gb[0], jnp.transpose(g2, (1, 0, 2)))


def solution(mesh):
    field, whole = P(None, "diag", "bins"), P()
    return jax.shard_map(
        shards, mesh=mesh, in_specs=(field, field, P("diag", "bins"), whole, whole, whole, whole),
        out_specs=(field, field, whole, whole, whole), check_vma=False)
```
